32 devices in a mesh: parts: 2 (over y), replica: 4 (over z), tensor: 4 (over x, core).
Axes of the slice: x: 2, y: 2, z: 4, core: 2. Of those that a mesh axis runs over, the one named last changes fastest.
Arguments:
- tokens: bfloat16 [4096, 8192], P(('parts', 'replica'), 'tensor'), parts along dimension 0, may hold values from -6 to 6
- value_weight: bfloat16 [8192, 512], P('tensor'), may hold values from -0.0625 to 0.0625
- down_factor: bfloat16 [256, 8192, 64], P(('parts', 'replica'), 'tensor'), parts along dimension 0, may hold values from -0.0625 to 0.0625
- up_factor: bfloat16 [256, 64, 512], P(('parts', 'replica'), None, 'tensor'), parts along dimension 0, may hold values from -0.75 to 0.75
- request_adapter: int32 [4096], P('parts'), parts along dimension 0, may hold values from 0 to 127, as said below
- adapter_slot_map: int32 [256], P('parts'), parts along dimension 0, may hold values from 0 to 127, as said below
Outputs:
- values_out: bfloat16 [4096, 512], P(('parts', 'replica'), 'tensor'), parts along dimension 0
The draws below stay inside these ranges and needn't reach their ends.
There are 2 independent parts, one for each index of `parts`. The reference program is written for one: setup_inputs(seed, part) draws one part's arguments, and reference() takes and returns one part's arrays. A program takes and returns all parts, laid end to end along the dimension named above; an argument that names none is the same for every part. Nothing has to cross between parts.
Inputs may be any that keep to these rules, and one draw needn't show every extreme that they name: `request_adapter`: replica r holds requests r * 512 to (r + 1) * 512 - 1, and pool slots r * 32 to (r + 1) * 32 - 1. Of the requests of one replica, at most 256 have adapters whose slots lie on one replica; in every draw some replicas receive exactly 256 from every replica. `adapter_slot_map`: A permutation.
All inputs are finite; a program needn't handle non-finite values.
Results may differ from the reference program's by a relative error of at most 0.0043.
Values may be sent and summed in bfloat16 or wider, within the bound.
No kernel may reach another device: no remote copies, remote signals or barrier semaphores. Data moves between devices by JAX's collectives and lax.ppermute only.
A program may use at most 128 MiB of HBM per device.

```python
import jax
import jax.numpy as jnp
from jax import lax

MODEL_WIDTH = 8192
ADAPTER_RANK = 64
ADP_DEV = 32
ROW_DEV = 512
VALUE_FEATURES = 512
ADAPTER_COUNT = 128
ROWS = 2048
CAP = 256


def pool_ordering(key):
    return jax.random.permutation(jax.random.fold_in(key, 11), ADAPTER_COUNT)


def draw_adapter_slot_map(key, part):
    ordering = pool_ordering(key)
    return ordering.astype(jnp.int32)


def draw_request_adapter(key, part):
    ordering = pool_ordering(key)
    key = jax.random.fold_in(key, 5)
    owner_count = ROWS // ROW_DEV
    slot_count = owner_count * CAP
    hot_count = max(1, owner_count // 8)
    owner_rank = jax.random.permutation(jax.random.fold_in(key, 1), owner_count)
    slot_owner = jnp.arange(slot_count) // CAP
    is_hot = jnp.take(owner_rank, slot_owner) < hot_count

    def one_block(index):
        block_key = jax.random.fold_in(key, index + 100)
        priority = jax.random.permutation(jax.random.fold_in(block_key, 1), slot_count)
        priority = priority - jnp.where(is_hot, slot_count, 0)
        chosen = jnp.argsort(priority)[:ROW_DEV]
        shuffle = jax.random.permutation(jax.random.fold_in(block_key, 2), ROW_DEV)
        chosen = jnp.take(chosen, shuffle)
        uniform_index = jax.random.randint(jax.random.fold_in(block_key, 3), (ROW_DEV,), 0, ADP_DEV)
        local_index = uniform_index * uniform_index // ADP_DEV
        return chosen // CAP * ADP_DEV + local_index
    pool_slots = jax.vmap(one_block)(jnp.arange(owner_count)).reshape(-1)
    inverse = jnp.argsort(ordering)
    return jnp.take(inverse, pool_slots).astype(jnp.int32)


def levels(rng, extent, pieces, low, top_value):
    level, own = 1.0, jax.random.fold_in(rng, 6)
    for dim, parts in pieces:
        heights = jnp.exp(jax.random.uniform(jax.random.fold_in(own, dim), (parts,), jnp.float32, low / len(pieces), top_value / len(pieces)))
        level = level * jnp.repeat(heights, extent[dim] // parts).reshape([-1 if axis == dim else 1 for axis in range(len(extent))])
    return level


def centred(key, dims, deviation, bound, cuts=(), dtype=jnp.bfloat16):
    factor_of = levels(key, dims, cuts, -0.22, 0.18) if cuts else 1.0
    drawn = jax.random.normal(key, dims, jnp.float32) * deviation * factor_of
    return jnp.minimum(jnp.maximum(drawn, -bound), bound).astype(dtype)


def setup_inputs(seed: int = 0, part: int = 0) -> dict:
    key_of = jax.random.split(jax.random.key(seed), 7)
    part_splits = jax.random.split(jax.random.fold_in(key_of[6], part), 7)
    tokens = centred(part_splits[0], (ROWS, MODEL_WIDTH), 1.0, 6.0, ((0, 4), (1, 4)))
    value_weight = centred(key_of[1], (MODEL_WIDTH, VALUE_FEATURES), MODEL_WIDTH ** -0.5, 0.0625, ((0, 4),))
    down_factor = centred(part_splits[2], (ADAPTER_COUNT, MODEL_WIDTH, ADAPTER_RANK), MODEL_WIDTH ** -0.5, 0.0625, ((0, 4), (1, 4)))
    up_factor = centred(part_splits[3], (ADAPTER_COUNT, ADAPTER_RANK, VALUE_FEATURES), ADAPTER_RANK ** -0.5, 0.75, ((0, 4), (2, 4)))
    request_adapter = draw_request_adapter(jax.random.fold_in(jax.random.fold_in(key_of[6], part), 71), part)
    adapter_slot_map = draw_adapter_slot_map(jax.random.fold_in(jax.random.fold_in(key_of[6], part), 71), part)
    return {"tokens": tokens, "value_weight": value_weight, "down_factor": down_factor, "up_factor": up_factor, "request_adapter": request_adapter, "adapter_slot_map": adapter_slot_map}


ADAPTER_SCALE = 0.5


def reference(tokens, value_weight, down_factor, up_factor, request_adapter, adapter_slot_map):
    base_output = jnp.dot(tokens, value_weight, preferred_element_type=jnp.float32)
    slot = jnp.take(adapter_slot_map, request_adapter).astype(jnp.int32)
    block_rows = 32
    token_blocks = tokens.reshape(ROWS // block_rows, block_rows, MODEL_WIDTH)
    slot_blocks = slot.reshape(ROWS // block_rows, block_rows)

    def one_block(pair):
        features, local_slot_ids = pair
        down_factor_rows = jnp.take(down_factor, local_slot_ids, axis=0).astype(jnp.float32)
        rank_projected = jnp.einsum("nd,ndr->nr", features.astype(jnp.float32), down_factor_rows)
        rank_projected = rank_projected.astype(jnp.bfloat16)
        up_factor_rows = jnp.take(up_factor, local_slot_ids, axis=0).astype(jnp.float32)
        adapter_delta = jnp.einsum("nr,nro->no", rank_projected.astype(jnp.float32), up_factor_rows)
        return adapter_delta.astype(jnp.bfloat16)

    delta_outputs = lax.map(one_block, (token_blocks, slot_blocks)).reshape(ROWS, VALUE_FEATURES)
    return (base_output + ADAPTER_SCALE * delta_outputs.astype(jnp.float32)).astype(jnp.bfloat16)
```

```python
import functools

import jax
import jax.numpy as jnp
from jax import lax
from jax.experimental import pallas as pl
from jax.experimental.pallas import tpu as pltpu
from jax.sharding import PartitionSpec as P

ADAPTER_SCALE = 0.5
MAX_OWNERS = 8
VMEM_BYTES = 40 * 1024 * 1024
NT = (((1,), (1,)), ((), ()))
TN = (((0,), (0,)), ((), ()))


def plain_body(tokens, value_weight, down_factor, up_factor, request_adapter, adapter_slot_map):
    row_count, quarter = tokens.shape
    owners = lax.axis_size("replica")
    local_adapters = down_factor.shape[0]
    output_piece = up_factor.shape[2]
    capacity = 2 * row_count // owners
    my_index = lax.axis_index("replica")
    pool_slot = jnp.take(adapter_slot_map, request_adapter)
    owner_grid = (pool_slot // local_adapters).reshape(owners, row_count)
    local_grid = (pool_slot % local_adapters).reshape(owners, row_count)
    my_owner = lax.dynamic_slice_in_dim(owner_grid, my_index, 1, 0)[0]
    owner_hot = (my_owner[:, None] == jnp.arange(owners)[None, :]).astype(jnp.int32)
    my_rank = jnp.sum(jnp.cumsum(owner_hot, axis=0) * owner_hot, axis=1) - 1
    position = my_owner * capacity + my_rank
    packer = (jnp.arange(owners * capacity)[:, None] == position[None, :]).astype(jnp.bfloat16)
    outgoing = jnp.dot(packer, tokens, preferred_element_type=jnp.float32).astype(jnp.bfloat16)
    outgoing = outgoing.reshape(owners, capacity, quarter)
    partial_base = jnp.dot(tokens, value_weight, preferred_element_type=jnp.float32)
    arrived = lax.all_to_all(outgoing, "replica", split_axis=0, concat_axis=0, tiled=True)
    mine = (owner_grid == my_index).astype(jnp.int32)
    recv_rank = jnp.cumsum(mine, axis=1) - 1
    selector = (
        (recv_rank[:, None, :] == jnp.arange(capacity)[None, :, None]) & (mine[:, None, :] > 0)
    ).astype(jnp.int32)
    slot_local = jnp.sum(selector * local_grid[:, None, :], axis=2).reshape(owners * capacity)
    sort_order = jnp.argsort(slot_local, stable=True)
    inverse_order = jnp.argsort(sort_order)
    group_row_count = jnp.sum(
        (slot_local[:, None] == jnp.arange(local_adapters)[None, :]).astype(jnp.int32), axis=0
    )
    rows_by_adapter = jnp.take(arrived.reshape(owners * capacity, quarter), sort_order, axis=0)
    partial_rank = lax.ragged_dot(
        rows_by_adapter, down_factor, group_row_count, preferred_element_type=jnp.float32
    )
    rank_projected = lax.psum(partial_rank, "tensor").astype(jnp.bfloat16)
    sorted_delta = lax.ragged_dot(
        rank_projected, up_factor, group_row_count, preferred_element_type=jnp.float32
    ).astype(jnp.bfloat16)
    adapter_delta = jnp.take(sorted_delta, inverse_order, axis=0).reshape(
        owners, capacity, output_piece
    )
    returned = lax.all_to_all(adapter_delta, "replica", split_axis=0, concat_axis=0, tiled=True)
    adapter_delta_rows = jnp.einsum(
        "pr,po->ro",
        packer,
        returned.reshape(owners * capacity, output_piece),
        preferred_element_type=jnp.float32,
    )
    local_base_output = lax.psum_scatter(partial_base, "tensor", scatter_dimension=1, tiled=True)
    return (local_base_output + ADAPTER_SCALE * adapter_delta_rows).astype(jnp.bfloat16)


def iota(shape, dim):
    return lax.broadcasted_iota(jnp.int32, shape, dim)


def hot(mask):
    return jnp.where(mask, 1.0, 0.0).astype(jnp.bfloat16)


def route_rows(request_ref, map_ref, owners, local_adapters):
    rows, adapters = request_ref.shape[1], map_ref.shape[1]
    slots = map_ref[...]
    slot_owner = lax.div(slots, jnp.int32(local_adapters))
    slot_local = slots - slot_owner * local_adapters + 1
    which = iota((8, adapters), 0)
    table = jnp.where(which == 0, slot_owner, jnp.where(which == 1, slot_local, 0))
    table = table.astype(jnp.float32).astype(jnp.bfloat16)
    owner, local, marks = [], [], []
    for source in range(owners):
        one_hot = hot(iota((adapters, rows), 0) == request_ref[source : source + 1, :])
        found = jnp.dot(table, one_hot, preferred_element_type=jnp.float32).astype(jnp.int32)
        owner.append(found[0:1])
        local.append(found[1:2])
        marks.append(jnp.where(iota((8, rows), 0) == found[0:1], 1.0, 0.0))
    marks = jnp.concatenate(marks, axis=0)
    before = hot(iota((rows, rows), 0) < iota((rows, rows), 1))
    ranks = jnp.dot(marks.astype(jnp.bfloat16), before, preferred_element_type=jnp.float32)
    return owner, local, marks, ranks


def pack_kernel(
    owners, local_adapters, me_ref, request_ref, map_ref, tokens_ref,
    first_ref, over_ref, place_ref, adapter_ref, branch_ref, packer_ref,
):
    rows = request_ref.shape[1]
    capacity = 2 * rows // owners
    half = capacity // 2

    @pl.when(pl.program_id(0) == 0)
    def _():
        me = me_ref[0]
        owner, local, marks, ranks = route_rows(request_ref, map_ref, owners, local_adapters)
        counts = jnp.sum(marks, axis=1, keepdims=True)
        most = counts[0:8]
        my_owner = jnp.zeros((1, rows), jnp.int32)
        my_rank = jnp.zeros((1, rows), jnp.float32)
        for source in range(owners):
            block = slice(8 * source, 8 * source + 8)
            most = jnp.maximum(most, counts[block])
            own_rank = jnp.sum(ranks[block] * marks[block], axis=0, keepdims=True)
            my_owner = jnp.where(me == source, owner[source], my_owner)
            my_rank = jnp.where(me == source, own_rank, my_rank)
            rank_here = jnp.sum(
                jnp.where(iota((8, rows), 0) == me, ranks[block], 0.0), axis=0, keepdims=True
            ).astype(jnp.int32)
            slot_of = jnp.where(owner[source] == me, rank_here, -1)
            selector = hot(iota((capacity, rows), 0) == slot_of)
            local_rows = jnp.broadcast_to(local[source], (8, rows)).astype(jnp.float32)
            found = lax.dot_general(
                local_rows.astype(jnp.bfloat16), selector, NT, preferred_element_type=jnp.float32
            ).astype(jnp.int32)
            low, high = source * half, (owners + source) * half
            adapter_ref[:, low : low + half] = found[:, :half] - 1
            adapter_ref[:, high : high + half] = found[:, half:] - 1
        my_rank = my_rank.astype(jnp.int32)
        over = jnp.where(most > half, 1, 0)
        many = jnp.sum(over)
        top = jnp.sum(over * iota((8, 1), 0))
        branch = jnp.where(many <= 1, top, owners)
        branch_ref[0] = branch
        place_ref[...] = jnp.broadcast_to(my_owner * capacity + my_rank, (8, rows))
        first = jnp.where(my_rank < half, my_owner * half + my_rank, -1)
        late = (my_owner == branch) & (my_rank >= half)
        packer_ref[: owners * half, :] = hot(iota((owners * half, rows), 0) == first)
        packer_ref[owners * half :, :] = hot(
            iota((half, rows), 0) == jnp.where(late, my_rank - half, -1)
        )

    packed = jnp.dot(packer_ref[...], tokens_ref[...], preferred_element_type=jnp.float32)
    packed = packed.astype(jnp.bfloat16)
    first_ref[...] = packed[: owners * half]
    over_ref[...] = packed[owners * half :]


def pack(me, request_grid, slot_map, tokens, local_adapters):
    owners, rows = request_grid.shape
    width = tokens.shape[1]
    half = rows // owners
    pieces = 4
    block = width // pieces
    whole = lambda shape: pl.BlockSpec(shape, lambda i: (0, 0))
    strip = lambda height: pl.BlockSpec((height, block), lambda i: (0, i))
    return pl.pallas_call(
        functools.partial(pack_kernel, owners, local_adapters),
        grid=(pieces,),
        in_specs=[
            pl.BlockSpec(memory_space=pltpu.SMEM),
            whole(request_grid.shape),
            whole(slot_map.shape),
            strip(rows),
        ],
        out_specs=[
            strip(owners * half),
            strip(half),
            whole((8, rows)),
            whole((8, 2 * owners * half)),
            pl.BlockSpec(memory_space=pltpu.SMEM),
        ],
        out_shape=[
            jax.ShapeDtypeStruct((owners * half, width), jnp.bfloat16),
            jax.ShapeDtypeStruct((half, width), jnp.bfloat16),
            jax.ShapeDtypeStruct((8, rows), jnp.int32),
            jax.ShapeDtypeStruct((8, 2 * owners * half), jnp.int32),
            jax.ShapeDtypeStruct((1,), jnp.int32),
        ],
        scratch_shapes=[pltpu.VMEM(((owners + 1) * half, rows), jnp.bfloat16)],
        compiler_params=pltpu.CompilerParams(vmem_limit_bytes=VMEM_BYTES),
        name="pack",
    )(me, request_grid, slot_map, tokens)


def down_kernel(owners, rank, adapters, *refs):
    adapter_ref, down_ref, first_ref = refs[:3]
    late_refs = refs[3 : 3 + owners]
    total_ref, rows_ref, sems = refs[3 + owners :]
    step = pl.program_id(0)
    half = late_refs[0].shape[0]

    @pl.when(step == 0)
    def _():
        copies = [pltpu.make_async_copy(first_ref, rows_ref.at[: owners * half], sems.at[0])]
        for source in range(owners):
            at = (owners + source) * half
            copies.append(
                pltpu.make_async_copy(
                    late_refs[source], rows_ref.at[at : at + half], sems.at[1 + source]
                )
            )
        for copy in copies:
            copy.start()
        for copy in copies:
            copy.wait()
        total_ref[...] = jnp.zeros_like(total_ref)

    products = lax.dot_general(
        down_ref[...], rows_ref[...], NT, preferred_element_type=jnp.float32
    )
    total = total_ref[...]
    for k in range(adapters):
        chosen = adapter_ref[0:1, :] == step * adapters + k
        total += jnp.where(chosen, products[k * rank : (k + 1) * rank], 0.0)
    total_ref[...] = total


def down(adapter_row, down_rows, first, late, rank):
    owners = len(late)
    half, width = late[0].shape
    slots = 2 * owners * half
    adapters = 4
    block = adapters * rank
    return pl.pallas_call(
        functools.partial(down_kernel, owners, rank, adapters),
        grid=(down_rows.shape[0] // block,),
        in_specs=[
            pl.BlockSpec((8, slots), lambda i: (0, 0)),
            pl.BlockSpec((block, width), lambda i: (i, 0)),
        ]
        + [pl.BlockSpec(memory_space=pl.ANY)] * (1 + owners),
        out_specs=pl.BlockSpec((rank, slots), lambda i: (0, 0)),
        out_shape=jax.ShapeDtypeStruct((rank, slots), jnp.float32),
        scratch_shapes=[
            pltpu.VMEM((slots, width), jnp.bfloat16),
            pltpu.SemaphoreType.DMA((1 + owners,)),
        ],
        compiler_params=pltpu.CompilerParams(vmem_limit_bytes=VMEM_BYTES),
        cost_estimate=pl.CostEstimate(
            flops=2 * slots * width * down_rows.shape[0],
            bytes_accessed=2 * width * (slots + down_rows.shape[0]),
            transcendentals=0,
        ),
        name="down",
    )(adapter_row, down_rows, first, *late)


def up_kernel(owners, rank, adapters, adapter_ref, up_ref, one_ref, two_ref, out_ref):
    low_rank = (one_ref[...] + two_ref[...]).astype(jnp.bfloat16).astype(jnp.float32)
    spread = jnp.concatenate(
        [jnp.where(adapter_ref[0:1, :] == k, low_rank, 0.0).astype(jnp.bfloat16) for k in range(adapters)],
        axis=0,
    )
    delta = lax.dot_general(up_ref[...], spread, TN, preferred_element_type=jnp.float32)
    delta = delta.astype(jnp.bfloat16)
    half = out_ref.shape[2] // 2
    for source in range(owners):
        low, high = source * half, (owners + source) * half
        out_ref[source, :, :half] = delta[:, low : low + half]
        out_ref[source, :, half:] = delta[:, high : high + half]


def up(adapter_row, up_rows, one, two, owners):
    rank, slots = one.shape
    piece = up_rows.shape[1]
    adapters = up_rows.shape[0] // rank
    return pl.pallas_call(
        functools.partial(up_kernel, owners, rank, adapters),
        out_shape=jax.ShapeDtypeStruct((owners, piece, slots // owners), jnp.bfloat16),
        compiler_params=pltpu.CompilerParams(vmem_limit_bytes=VMEM_BYTES),
        name="up",
    )(adapter_row, up_rows, one, two)


def unpack_kernel(owners, place_ref, returned_ref, base_ref, out_ref):
    rows, capacity = base_ref.shape[0], returned_ref.shape[2]
    total = jnp.zeros((returned_ref.shape[1], rows), jnp.float32)
    for owner in range(owners):
        selector = hot(iota((capacity, rows), 0) == place_ref[0:1, :] - owner * capacity)
        total += jnp.dot(returned_ref[owner], selector, preferred_element_type=jnp.float32)
    out_ref[...] = (base_ref[...] + ADAPTER_SCALE * total.T).astype(jnp.bfloat16)


def unpack(place, returned, base):
    return pl.pallas_call(
        functools.partial(unpack_kernel, returned.shape[0]),
        out_shape=jax.ShapeDtypeStruct(base.shape, jnp.bfloat16),
        compiler_params=pltpu.CompilerParams(vmem_limit_bytes=VMEM_BYTES),
        name="unpack",
    )(place, returned, base)


def exchange(array, axis, bit):
    size = lax.axis_size(axis)
    return lax.ppermute(array, axis, [(k, k ^ bit) for k in range(size)])


def body(tokens, value_weight, down_factor, up_factor, request_adapter, adapter_slot_map):
    row_count, quarter = tokens.shape
    owners = lax.axis_size("replica")
    local_adapters, _, rank = down_factor.shape
    half = row_count // owners
    me = lax.axis_index("replica").astype(jnp.int32).reshape(1)
    request_grid = request_adapter.reshape(owners, row_count)
    slot_map = adapter_slot_map.reshape(1, -1)
    down_rows = jnp.swapaxes(down_factor, 1, 2).reshape(local_adapters * rank, quarter)
    up_rows = up_factor.reshape(local_adapters * rank, -1)

    first, over, place, adapter_row, branch = pack(
        me, request_grid, slot_map, tokens, local_adapters
    )
    first = first.reshape(owners, half, quarter)
    arrived = lax.all_to_all(first, "replica", split_axis=0, concat_axis=0, tiled=True)

    def to_one(owner):
        def send(over, place, tokens):
            return tuple(
                over if source == owner else lax.ppermute(over, "replica", [(source, owner)])
                for source in range(owners)
            )

        return send

    def to_all(over, place, tokens):
        spot = place[0]
        owner, late = spot // (2 * half), spot % (2 * half) - half
        index = jnp.where(late >= 0, owner * half + late, -1)
        packer = (jnp.arange(owners * half)[:, None] == index[None, :]).astype(jnp.bfloat16)
        outgoing = jnp.dot(packer, tokens, preferred_element_type=jnp.float32)
        outgoing = outgoing.astype(jnp.bfloat16).reshape(owners, half, quarter)
        came = lax.all_to_all(outgoing, "replica", split_axis=0, concat_axis=0, tiled=True)
        return tuple(came[source] for source in range(owners))

    late = lax.switch(
        branch[0], [to_one(owner) for owner in range(owners)] + [to_all], over, place, tokens
    )
    partial_base = jnp.dot(tokens, value_weight, preferred_element_type=jnp.float32)
    base = lax.psum_scatter(partial_base, "tensor", scatter_dimension=1, tiled=True)

    one = down(adapter_row, down_rows, arrived.reshape(owners * half, quarter), late, rank)
    bits = [1 << k for k in range((lax.axis_size("tensor") - 1).bit_length())]
    two = exchange(one, "tensor", bits[0])
    for bit in bits[1:]:
        one = one + two
        two = exchange(one, "tensor", bit)
    delta = up(adapter_row, up_rows, one, two, owners)
    returned = lax.all_to_all(delta, "replica", split_axis=0, concat_axis=0, tiled=True)
    return unpack(place, returned, base)


def solution(mesh):
    in_specs = (
        P(("parts", "replica"), "tensor"),
        P("tensor", None),
        P(("parts", "replica"), "tensor", None),
        P(("parts", "replica"), None, "tensor"),
        P("parts"),
        P("parts"),
    )
    out_specs = P(("parts", "replica"), "tensor")
    chosen = body if mesh.shape["replica"] <= MAX_OWNERS else plain_body
    return jax.shard_map(chosen, mesh=mesh, in_specs=in_specs, out_specs=out_specs, check_vma=False)
```

```python
import functools

import jax
import jax.numpy as jnp
from jax import lax
from jax.experimental import pallas as pl
from jax.experimental.pallas import tpu as pltpu
from jax.sharding import PartitionSpec as P

ADAPTER_SCALE = 0.5
MAX_OWNERS = 8
VMEM_BYTES = 40 * 1024 * 1024
NT = (((1,), (1,)), ((), ()))
TN = (((0,), (0,)), ((), ()))


def plain_body(tokens, value_weight, down_factor, up_factor, request_adapter, adapter_slot_map):
    row_count, quarter = tokens.shape
    owners = lax.axis_size("replica")
    local_adapters = down_factor.shape[0]
    output_piece = up_factor.shape[2]
    capacity = 2 * row_count // owners
    my_index = lax.axis_index("replica")
    pool_slot = jnp.take(adapter_slot_map, request_adapter)
    owner_grid = (pool_slot // local_adapters).reshape(owners, row_count)
    local_grid = (pool_slot % local_adapters).reshape(owners, row_count)
    my_owner = lax.dynamic_slice_in_dim(owner_grid, my_index, 1, 0)[0]
    owner_hot = (my_owner[:, None] == jnp.arange(owners)[None, :]).astype(jnp.int32)
    my_rank = jnp.sum(jnp.cumsum(owner_hot, axis=0) * owner_hot, axis=1) - 1
    position = my_owner * capacity + my_rank
    packer = (jnp.arange(owners * capacity)[:, None] == position[None, :]).astype(jnp.bfloat16)
    outgoing = jnp.dot(packer, tokens, preferred_element_type=jnp.float32).astype(jnp.bfloat16)
    outgoing = outgoing.reshape(owners, capacity, quarter)
    partial_base = jnp.dot(tokens, value_weight, preferred_element_type=jnp.float32)
    arrived = lax.all_to_all(outgoing, "replica", split_axis=0, concat_axis=0, tiled=True)
    mine = (owner_grid == my_index).astype(jnp.int32)
    recv_rank = jnp.cumsum(mine, axis=1) - 1
    selector = (
        (recv_rank[:, None, :] == jnp.arange(capacity)[None, :, None]) & (mine[:, None, :] > 0)
    ).astype(jnp.int32)
    slot_local = jnp.sum(selector * local_grid[:, None, :], axis=2).reshape(owners * capacity)
    sort_order = jnp.argsort(slot_local, stable=True)
    inverse_order = jnp.argsort(sort_order)
    group_row_count = jnp.sum(
        (slot_local[:, None] == jnp.arange(local_adapters)[None, :]).astype(jnp.int32), axis=0
    )
    rows_by_adapter = jnp.take(arrived.reshape(owners * capacity, quarter), sort_order, axis=0)
    partial_rank = lax.ragged_dot(
        rows_by_adapter, down_factor, group_row_count, preferred_element_type=jnp.float32
    )
    rank_projected = lax.psum(partial_rank, "tensor").astype(jnp.bfloat16)
    sorted_delta = lax.ragged_dot(
        rank_projected, up_factor, group_row_count, preferred_element_type=jnp.float32
    ).astype(jnp.bfloat16)
    adapter_delta = jnp.take(sorted_delta, inverse_order, axis=0).reshape(
        owners, capacity, output_piece
    )
    returned = lax.all_to_all(adapter_delta, "replica", split_axis=0, concat_axis=0, tiled=True)
    adapter_delta_rows = jnp.einsum(
        "pr,po->ro",
        packer,
        returned.reshape(owners * capacity, output_piece),
        preferred_element_type=jnp.float32,
    )
    local_base_output = lax.psum_scatter(partial_base, "tensor", scatter_dimension=1, tiled=True)
    return (local_base_output + ADAPTER_SCALE * adapter_delta_rows).astype(jnp.bfloat16)


def iota(shape, dim):
    return lax.broadcasted_iota(jnp.int32, shape, dim)


def hot(mask):
    return jnp.where(mask, 1.0, 0.0).astype(jnp.bfloat16)


def lookup(request_ref, map_ref, owners, local_adapters):
    rows, adapters = request_ref.shape[1], map_ref.shape[1]
    slots = map_ref[...]
    which = iota((16, adapters), 0)
    owner = lax.div(slots, jnp.int32(local_adapters))
    table = jnp.where(which == 8, slots, jnp.where(which == owner, 1, 0))
    table = table.astype(jnp.float32).astype(jnp.bfloat16)
    one_hot = hot(iota((adapters, rows), 0) == request_ref[...])
    found = jnp.dot(table, one_hot, preferred_element_type=jnp.float32)
    return found[8:9].astype(jnp.int32), found[0:8]


def column_sums(table, counts):
    wide = jnp.broadcast_to(counts, (counts.shape[0], 128)).astype(jnp.bfloat16)
    return jnp.dot(table, wide, preferred_element_type=jnp.float32)[:, :1]


def pack_kernel(
    owners, local_adapters, me_ref, request_ref, map_ref, tokens_ref,
    first_ref, over_ref, place_ref, branch_ref, packer_ref,
):
    rows = tokens_ref.shape[0]
    capacity = 2 * rows // owners
    half = capacity // 2
    pool = map_ref.shape[1]

    @pl.when(pl.program_id(0) == 0)
    def _():
        me = me_ref[0]
        slots, marks = lookup(request_ref, map_ref, owners, local_adapters)
        most = jnp.zeros((8, 1), jnp.float32)
        slot = jnp.zeros((1, rows), jnp.int32)
        for source in range(owners):
            span = slice(source * rows, (source + 1) * rows)
            most = jnp.maximum(most, jnp.sum(marks[:, span], axis=1, keepdims=True))
            slot = jnp.where(me == source, slots[:, span], slot)
        over = jnp.where(most > half, 1, 0)
        branch = jnp.where(jnp.sum(over) <= 1, jnp.sum(over * iota((8, 1), 0)), owners)
        branch_ref[0] = branch
        mine = iota((pool, rows), 0) == slot
        one_hot = hot(mine)
        before = hot(iota((rows, rows), 0) < iota((rows, rows), 1))
        ranks = jnp.dot(one_hot, before, preferred_element_type=jnp.float32)
        counts = jnp.sum(jnp.where(mine, 1.0, 0.0), axis=1, keepdims=True)
        row, column = iota((pool, pool), 0), iota((pool, pool), 1)
        same = lax.div(row, jnp.int32(local_adapters)) == lax.div(column, jnp.int32(local_adapters))
        ranks += column_sums(hot(same & (column < row)), counts)
        rank = jnp.sum(jnp.where(mine, ranks, 0.0), axis=0, keepdims=True).astype(jnp.int32)
        owner = lax.div(slot, jnp.int32(local_adapters))
        place_ref[...] = jnp.broadcast_to(owner * capacity + rank, (8, rows))
        first = jnp.where(rank < half, owner * half + rank, -1)
        target = jnp.where(branch < owners, branch, me)
        late = jnp.where((owner == target) & (rank >= half), rank - half, -1)
        packer_ref[: owners * half, :] = hot(iota((owners * half, rows), 0) == first)
        packer_ref[owners * half :, :] = hot(iota((half, rows), 0) == late)

    packed = jnp.dot(packer_ref[...], tokens_ref[...], preferred_element_type=jnp.float32)
    packed = packed.astype(jnp.bfloat16)
    first_ref[...] = packed[: owners * half]
    over_ref[...] = packed[owners * half :]


def pack(me, requests, slot_map, tokens, owners, local_adapters):
    rows, width = tokens.shape
    half = rows // owners
    pieces = 4
    block = width // pieces
    whole = lambda shape: pl.BlockSpec(shape, lambda i: (0, 0))
    strip = lambda height: pl.BlockSpec((height, block), lambda i: (0, i))
    return pl.pallas_call(
        functools.partial(pack_kernel, owners, local_adapters),
        grid=(pieces,),
        in_specs=[
            pl.BlockSpec(memory_space=pltpu.SMEM),
            whole(requests.shape),
            whole(slot_map.shape),
            strip(rows),
        ],
        out_specs=[
            strip(owners * half),
            strip(half),
            whole((8, rows)),
            pl.BlockSpec(memory_space=pltpu.SMEM),
        ],
        out_shape=[
            pltpu.HBM((owners * half, width), jnp.bfloat16),
            pltpu.HBM((half, width), jnp.bfloat16),
            jax.ShapeDtypeStruct((8, rows), jnp.int32),
            jax.ShapeDtypeStruct((1,), jnp.int32),
        ],
        scratch_shapes=[pltpu.VMEM(((owners + 1) * half, rows), jnp.bfloat16)],
        compiler_params=pltpu.CompilerParams(vmem_limit_bytes=VMEM_BYTES),
        name="pack",
    )(me, requests, slot_map, tokens)


def plan_kernel(
    owners, local_adapters, rows, me_ref, request_ref, map_ref, adapter_ref, bound_ref
):
    me = me_ref[0]
    capacity = 2 * rows // owners
    half = capacity // 2
    slots, _ = lookup(request_ref, map_ref, owners, local_adapters)
    row, column = iota((local_adapters, local_adapters), 0), iota((local_adapters, local_adapters), 1)
    upto = hot(column <= row)
    place = iota((local_adapters, capacity), 1)
    for source in range(owners):
        slot = slots[:, source * rows : (source + 1) * rows]
        mine = iota((local_adapters, rows), 0) + me * local_adapters == slot
        counts = jnp.sum(jnp.where(mine, 1.0, 0.0), axis=1, keepdims=True)
        ends = column_sums(upto, counts).astype(jnp.int32)
        passed = jnp.sum(jnp.where(ends <= place, 1, 0), axis=0, keepdims=True)
        adapter = jnp.where(passed < local_adapters, passed, -1)
        adapter = jnp.broadcast_to(adapter, (8, capacity))
        adapter_ref[:, source * half : (source + 1) * half] = adapter[:, :half]
        shift = lax.rem(me - source + owners, owners)
        start = pl.multiple_of((owners + shift) * half, half)
        adapter_ref[:, pl.ds(start, half)] = adapter[:, half:]
    for part in range(2):
        found = adapter_ref[:, part * owners * half : (part + 1) * owners * half]
        bound_ref[2 * part] = jnp.min(jnp.where(found < 0, local_adapters, found))
        bound_ref[2 * part + 1] = jnp.max(found)


def plan(me, requests, slot_map, owners, local_adapters):
    rows = requests.shape[1] // owners
    vmem, smem = pl.BlockSpec(memory_space=pltpu.VMEM), pl.BlockSpec(memory_space=pltpu.SMEM)
    return pl.pallas_call(
        functools.partial(plan_kernel, owners, local_adapters, rows),
        in_specs=[smem, vmem, vmem],
        out_specs=[vmem, smem],
        out_shape=[
            jax.ShapeDtypeStruct((8, 2 * rows), jnp.int32),
            jax.ShapeDtypeStruct((4,), jnp.int32),
        ],
        compiler_params=pltpu.CompilerParams(vmem_limit_bytes=VMEM_BYTES),
        name="plan",
    )(me, requests, slot_map)


def down_kernel(part, rank, adapters, count, *refs):
    bound_ref, adapter_ref, down_ref = refs[:3]
    sent_refs = refs[3 : 3 + count]
    total_ref, rows_ref, sems = refs[3 + count :]
    step = pl.program_id(0)

    @pl.when(step == 0)
    def _():
        size = sent_refs[0].shape[0]
        copies = [
            pltpu.make_async_copy(ref, rows_ref.at[k * size : (k + 1) * size], sems.at[k])
            for k, ref in enumerate(sent_refs)
        ]
        for copy in copies:
            copy.start()
        total_ref[...] = jnp.zeros_like(total_ref)
        for copy in copies:
            copy.wait()

    low = step * adapters

    @pl.when((bound_ref[2 * part] < low + adapters) & (bound_ref[2 * part + 1] >= low))
    def _():
        products = lax.dot_general(
            down_ref[...], rows_ref[...], NT, preferred_element_type=jnp.float32
        )
        total = total_ref[...]
        for k in range(adapters):
            chosen = adapter_ref[0:1, :] == low + k
            total += jnp.where(chosen, products[k * rank : (k + 1) * rank], 0.0)
        total_ref[...] = total


def down(part, bounds, adapter_row, down_rows, sent, rank):
    width = sent[0].shape[1]
    slots = adapter_row.shape[1] // 2
    adapters = 4
    block = adapters * rank
    return pl.pallas_call(
        functools.partial(down_kernel, part, rank, adapters, len(sent)),
        grid=(down_rows.shape[0] // block,),
        in_specs=[
            pl.BlockSpec(memory_space=pltpu.SMEM),
            pl.BlockSpec((8, slots), lambda i: (0, part)),
            pl.BlockSpec((block, width), lambda i: (i, 0)),
        ]
        + [pl.BlockSpec(memory_space=pl.ANY)] * len(sent),
        out_specs=pl.BlockSpec((rank, slots), lambda i: (0, 0)),
        out_shape=jax.ShapeDtypeStruct((rank, slots), jnp.float32),
        scratch_shapes=[
            pltpu.VMEM((slots, width), jnp.bfloat16),
            pltpu.SemaphoreType.DMA((len(sent),)),
        ],
        compiler_params=pltpu.CompilerParams(vmem_limit_bytes=VMEM_BYTES),
        cost_estimate=pl.CostEstimate(
            flops=slots * width * down_rows.shape[0],
            bytes_accessed=2 * width * (slots + down_rows.shape[0]),
            transcendentals=0,
        ),
        name="down",
    )(bounds, adapter_row, pltpu.with_memory_space_constraint(down_rows, pltpu.HBM), *sent)


def up_kernel(owners, rank, adapters, me_ref, side_ref, adapter_ref, up_ref, mine_ref, other_ref, out_ref):
    me, side = me_ref[0], side_ref[0]
    mine, other = mine_ref[...].astype(jnp.float32), other_ref[...].astype(jnp.float32)
    wide = mine.shape[1]
    half = wide // owners
    for part in range(2):
        low_rank = jnp.where(side == part, mine, other)
        chosen = adapter_ref[0:1, part * wide : (part + 1) * wide]
        spread = jnp.concatenate(
            [jnp.where(chosen == k, low_rank, 0.0).astype(jnp.bfloat16) for k in range(adapters)],
            axis=0,
        )
        delta = lax.dot_general(up_ref[...], spread, TN, preferred_element_type=jnp.float32)
        delta = delta.astype(jnp.bfloat16)
        for k in range(owners):
            source = k if part == 0 else lax.rem(me - k + owners, owners)
            out_ref[source, :, part * half : (part + 1) * half] = delta[:, k * half : (k + 1) * half]


def up(me, side, adapter_row, up_rows, mine, other, owners):
    rank, wide = mine.shape
    piece = up_rows.shape[1]
    adapters = up_rows.shape[0] // rank
    vmem, smem = pl.BlockSpec(memory_space=pltpu.VMEM), pl.BlockSpec(memory_space=pltpu.SMEM)
    return pl.pallas_call(
        functools.partial(up_kernel, owners, rank, adapters),
        in_specs=[smem, smem, vmem, vmem, vmem, vmem],
        out_shape=jax.ShapeDtypeStruct((owners, piece, 2 * wide // owners), jnp.bfloat16),
        compiler_params=pltpu.CompilerParams(vmem_limit_bytes=VMEM_BYTES),
        name="up",
    )(me, side, adapter_row, up_rows, mine, other)


def unpack_kernel(owners, place_ref, returned_ref, *refs):
    base_refs, out_ref = refs[:-1], refs[-1]
    rows, capacity = out_ref.shape[0], returned_ref.shape[2]
    total = jnp.zeros((returned_ref.shape[1], rows), jnp.float32)
    for owner in range(owners):
        selector = hot(iota((capacity, rows), 0) == place_ref[0:1, :] - owner * capacity)
        total += jnp.dot(returned_ref[owner], selector, preferred_element_type=jnp.float32)
    base = base_refs[0][...]
    for base_ref in base_refs[1:]:
        base += base_ref[...]
    out_ref[...] = (base + ADAPTER_SCALE * total.T).astype(jnp.bfloat16)


def unpack(place, returned, base):
    return pl.pallas_call(
        functools.partial(unpack_kernel, returned.shape[0]),
        out_shape=jax.ShapeDtypeStruct(base[0].shape, jnp.bfloat16),
        compiler_params=pltpu.CompilerParams(vmem_limit_bytes=VMEM_BYTES),
        name="unpack",
    )(place, returned, *base)


def exchange(array, axis, bit):
    size = lax.axis_size(axis)
    return lax.ppermute(array, axis, [(k, k ^ bit) for k in range(size)])


def body(tokens, value_weight, down_factor, up_factor, request_adapter, adapter_slot_map):
    row_count, quarter = tokens.shape
    owners = lax.axis_size("replica")
    tensor = lax.axis_size("tensor")
    local_adapters, _, rank = down_factor.shape
    half = row_count // owners
    me = lax.axis_index("replica").astype(jnp.int32).reshape(1)
    side = (lax.axis_index("tensor").astype(jnp.int32) % 2).reshape(1)
    requests = request_adapter.reshape(1, -1)
    slot_map = adapter_slot_map.reshape(1, -1)
    down_rows = jnp.swapaxes(down_factor, 1, 2).reshape(local_adapters * rank, quarter)
    up_rows = up_factor.reshape(local_adapters * rank, -1)

    first, over, place, branch = pack(me, requests, slot_map, tokens, owners, local_adapters)
    first = first.reshape(owners, half, quarter)
    piece = value_weight.shape[1] // tensor

    def work(late, first, over, tokens, value_weight, down_rows, requests, slot_map):
        arrived = lax.all_to_all(first, "replica", split_axis=0, concat_axis=0, tiled=True)
        base = []
        for bit in range(tensor):
            column = (lax.axis_index("tensor") ^ bit) * piece
            part = jnp.dot(
                tokens,
                lax.dynamic_slice_in_dim(value_weight, column, piece, 1),
                preferred_element_type=jnp.float32,
            )
            base.append(part if bit == 0 else exchange(part, "tensor", bit))
        adapter_row, bounds = plan(me, requests, slot_map, owners, local_adapters)
        one = down(
            0, bounds, adapter_row, down_rows, (arrived.reshape(owners * half, quarter),), rank
        )
        two = down(1, bounds, adapter_row, down_rows, (over, *late), rank)
        return one, two, adapter_row, *base

    def to_one(owner):
        def send(place, first, over, tokens, *rest):
            late = tuple(
                lax.ppermute(over, "replica", [((owner - shift) % owners, owner)])
                for shift in range(1, owners)
            )
            return work(late, first, over, tokens, *rest)

        return send

    def to_all(place, first, over, tokens, *rest):
        spot = place[0]
        owner, late = spot // (2 * half), spot % (2 * half) - half
        index = jnp.where(late >= 0, owner * half + late, -1)
        packer = (jnp.arange(owners * half)[:, None] == index[None, :]).astype(jnp.bfloat16)
        outgoing = jnp.dot(packer, tokens, preferred_element_type=jnp.float32)
        outgoing = outgoing.astype(jnp.bfloat16).reshape(owners, half, quarter)
        came = lax.all_to_all(outgoing, "replica", split_axis=0, concat_axis=0, tiled=True)
        here = lax.axis_index("replica")
        late = tuple(
            lax.dynamic_index_in_dim(came, (here - shift) % owners, 0, keepdims=False)
            for shift in range(1, owners)
        )
        return work(late, first, over, tokens, *rest)

    one, two, adapter_row, *base = lax.switch(
        branch[0],
        [to_one(owner) for owner in range(owners)] + [to_all],
        place, first, over, tokens, value_weight, down_rows, requests, slot_map,
    )
    keep = jnp.where(side[0] == 0, one, two)
    give = jnp.where(side[0] == 0, two, one)
    keep = keep + exchange(give, "tensor", 1)
    bit = 2
    while bit < tensor:
        keep = keep + exchange(keep, "tensor", bit)
        bit *= 2
    mine = keep.astype(jnp.bfloat16)
    other = exchange(mine, "tensor", 1)
    delta = up(me, side, adapter_row, up_rows, mine, other, owners)
    returned = lax.all_to_all(delta, "replica", split_axis=0, concat_axis=0, tiled=True)
    return unpack(place, returned, base)


def solution(mesh):
    in_specs = (
        P(("parts", "replica"), "tensor"),
        P("tensor", None),
        P(("parts", "replica"), "tensor", None),
        P(("parts", "replica"), None, "tensor"),
        P("parts"),
        P("parts"),
    )
    out_specs = P(("parts", "replica"), "tensor")
    chosen = body if mesh.shape["replica"] <= MAX_OWNERS else plain_body
    return jax.shard_map(chosen, mesh=mesh, in_specs=in_specs, out_specs=out_specs, check_vma=False)
```

```python
import functools

import jax
import jax.numpy as jnp
from jax import lax
from jax.experimental import pallas as pl
from jax.experimental.pallas import tpu as pltpu
from jax.sharding import PartitionSpec as P

ADAPTER_SCALE = 0.5
MAX_OWNERS = 8
COPIES = 8
GROUPS = 4
BLOCK = 4
BRIEF = pl.CostEstimate(flops=0, bytes_accessed=0, transcendentals=0)
VMEM_BYTES = 40 * 1024 * 1024
NT = (((1,), (1,)), ((), ()))
TN = (((0,), (0,)), ((), ()))


def plain_body(tokens, value_weight, down_factor, up_factor, request_adapter, adapter_slot_map):
    row_count, quarter = tokens.shape
    owners = lax.axis_size("replica")
    local_adapters = down_factor.shape[0]
    output_piece = up_factor.shape[2]
    capacity = 2 * row_count // owners
    my_index = lax.axis_index("replica")
    pool_slot = jnp.take(adapter_slot_map, request_adapter)
    owner_grid = (pool_slot // local_adapters).reshape(owners, row_count)
    local_grid = (pool_slot % local_adapters).reshape(owners, row_count)
    my_owner = lax.dynamic_slice_in_dim(owner_grid, my_index, 1, 0)[0]
    owner_hot = (my_owner[:, None] == jnp.arange(owners)[None, :]).astype(jnp.int32)
    my_rank = jnp.sum(jnp.cumsum(owner_hot, axis=0) * owner_hot, axis=1) - 1
    position = my_owner * capacity + my_rank
    packer = (jnp.arange(owners * capacity)[:, None] == position[None, :]).astype(jnp.bfloat16)
    outgoing = jnp.dot(packer, tokens, preferred_element_type=jnp.float32).astype(jnp.bfloat16)
    outgoing = outgoing.reshape(owners, capacity, quarter)
    partial_base = jnp.dot(tokens, value_weight, preferred_element_type=jnp.float32)
    arrived = lax.all_to_all(outgoing, "replica", split_axis=0, concat_axis=0, tiled=True)
    mine = (owner_grid == my_index).astype(jnp.int32)
    recv_rank = jnp.cumsum(mine, axis=1) - 1
    selector = (
        (recv_rank[:, None, :] == jnp.arange(capacity)[None, :, None]) & (mine[:, None, :] > 0)
    ).astype(jnp.int32)
    slot_local = jnp.sum(selector * local_grid[:, None, :], axis=2).reshape(owners * capacity)
    sort_order = jnp.argsort(slot_local, stable=True)
    inverse_order = jnp.argsort(sort_order)
    group_row_count = jnp.sum(
        (slot_local[:, None] == jnp.arange(local_adapters)[None, :]).astype(jnp.int32), axis=0
    )
    rows_by_adapter = jnp.take(arrived.reshape(owners * capacity, quarter), sort_order, axis=0)
    partial_rank = lax.ragged_dot(
        rows_by_adapter, down_factor, group_row_count, preferred_element_type=jnp.float32
    )
    rank_projected = lax.psum(partial_rank, "tensor").astype(jnp.bfloat16)
    sorted_delta = lax.ragged_dot(
        rank_projected, up_factor, group_row_count, preferred_element_type=jnp.float32
    ).astype(jnp.bfloat16)
    adapter_delta = jnp.take(sorted_delta, inverse_order, axis=0).reshape(
        owners, capacity, output_piece
    )
    returned = lax.all_to_all(adapter_delta, "replica", split_axis=0, concat_axis=0, tiled=True)
    adapter_delta_rows = jnp.einsum(
        "pr,po->ro",
        packer,
        returned.reshape(owners * capacity, output_piece),
        preferred_element_type=jnp.float32,
    )
    local_base_output = lax.psum_scatter(partial_base, "tensor", scatter_dimension=1, tiled=True)
    return (local_base_output + ADAPTER_SCALE * adapter_delta_rows).astype(jnp.bfloat16)


def iota(shape, dim):
    return lax.broadcasted_iota(jnp.int32, shape, dim)


def hot(mask):
    return jnp.where(mask, 1.0, 0.0).astype(jnp.bfloat16)


def lookup(request_ref, map_ref, owners, local_adapters):
    rows, adapters = request_ref.shape[1], map_ref.shape[1]
    slots = map_ref[...]
    which = iota((16, adapters), 0)
    owner = lax.div(slots, jnp.int32(local_adapters))
    table = jnp.where(which == 8, slots, jnp.where(which == owner, 1, 0))
    table = table.astype(jnp.float32).astype(jnp.bfloat16)
    one_hot = hot(iota((adapters, rows), 0) == request_ref[...])
    found = jnp.dot(table, one_hot, preferred_element_type=jnp.float32)
    return found[8:9].astype(jnp.int32), found[0:8]


def column_sums(table, counts):
    wide = jnp.broadcast_to(counts, (counts.shape[0], 128)).astype(jnp.bfloat16)
    return jnp.dot(table, wide, preferred_element_type=jnp.float32)[:, :1]


def start_copies(source_ref, target_ref, sems, offset=0):
    size = source_ref.shape[0] // sems.shape[0]
    copies = [
        pltpu.make_async_copy(
            source_ref.at[k * size : (k + 1) * size],
            target_ref.at[offset + k * size : offset + (k + 1) * size],
            sems.at[k],
        )
        for k in range(sems.shape[0])
    ]
    for copy in copies:
        copy.start()
    return copies


def route_kernel(
    owners, local_adapters, me_ref, request_ref, map_ref, tokens_ref,
    first_ref, over_ref, place_ref, branch_ref, rows_ref, packed_ref, sems, out_sems,
):
    rows, width = tokens_ref.shape
    capacity = 2 * rows // owners
    half = capacity // 2
    pool = map_ref.shape[1]
    copies = start_copies(tokens_ref, rows_ref, sems)
    me = me_ref[0]
    slots, marks = lookup(request_ref, map_ref, owners, local_adapters)
    most = jnp.zeros((8, 1), jnp.float32)
    slot = jnp.zeros((1, rows), jnp.int32)
    for source in range(owners):
        span = slice(source * rows, (source + 1) * rows)
        most = jnp.maximum(most, jnp.sum(marks[:, span], axis=1, keepdims=True))
        slot = jnp.where(me == source, slots[:, span], slot)
    over = jnp.where(most > half, 1, 0)
    branch = jnp.where(jnp.sum(over) <= 1, jnp.sum(over * iota((8, 1), 0)), owners)
    branch_ref[0] = branch
    mine = iota((pool, rows), 0) == slot
    one_hot = hot(mine)
    before = hot(iota((rows, rows), 0) < iota((rows, rows), 1))
    ranks = jnp.dot(one_hot, before, preferred_element_type=jnp.float32)
    counts = jnp.sum(jnp.where(mine, 1.0, 0.0), axis=1, keepdims=True)
    row, column = iota((pool, pool), 0), iota((pool, pool), 1)
    same = lax.div(row, jnp.int32(local_adapters)) == lax.div(column, jnp.int32(local_adapters))
    ranks += column_sums(hot(same & (column < row)), counts)
    rank = jnp.sum(jnp.where(mine, ranks, 0.0), axis=0, keepdims=True).astype(jnp.int32)
    owner = lax.div(slot, jnp.int32(local_adapters))
    place_ref[...] = jnp.broadcast_to(owner * capacity + rank, (8, rows))
    target = jnp.where(branch < owners, branch, me)
    late = jnp.where((owner == target) & (rank >= half), rank - half, -1)
    first = jnp.where(rank < half, owner * half + rank, -1)
    for copy in copies:
        copy.wait()
    sends = []
    for k in range(owners + 1):
        index = late if k == 0 else first - (k - 1) * half
        packer = hot(iota((half, rows), 0) == index)
        packed = jnp.dot(packer, rows_ref[...], preferred_element_type=jnp.float32)
        packed_ref[k * half : (k + 1) * half, :] = packed.astype(jnp.bfloat16)
        target_ref = over_ref if k == 0 else first_ref.at[(k - 1) * half : k * half]
        sends.append(
            pltpu.make_async_copy(packed_ref.at[k * half : (k + 1) * half], target_ref, out_sems.at[k])
        )
        sends[-1].start()
    for send in sends:
        send.wait()


def route(me, requests, slot_map, tokens, owners, local_adapters):
    rows, width = tokens.shape
    half = rows // owners
    vmem, smem = pl.BlockSpec(memory_space=pltpu.VMEM), pl.BlockSpec(memory_space=pltpu.SMEM)
    anywhere = pl.BlockSpec(memory_space=pl.ANY)
    return pl.pallas_call(
        functools.partial(route_kernel, owners, local_adapters),
        in_specs=[smem, vmem, vmem, anywhere],
        out_specs=[anywhere, anywhere, vmem, smem],
        out_shape=[
            pltpu.HBM((rows, width), jnp.bfloat16),
            pltpu.HBM((half, width), jnp.bfloat16),
            jax.ShapeDtypeStruct((8, rows), jnp.int32),
            jax.ShapeDtypeStruct((1,), jnp.int32),
        ],
        scratch_shapes=[
            pltpu.VMEM((rows, width), jnp.bfloat16),
            pltpu.VMEM((rows + half, width), jnp.bfloat16),
            pltpu.SemaphoreType.DMA((COPIES,)),
            pltpu.SemaphoreType.DMA((owners + 1,)),
        ],
        compiler_params=pltpu.CompilerParams(vmem_limit_bytes=VMEM_BYTES),
        name="route",
    )(me, requests, slot_map, tokens)


def plan_kernel(
    owners, local_adapters, rows, me_ref, request_ref, map_ref, adapter_ref, bound_ref
):
    me = me_ref[0]
    capacity = 2 * rows // owners
    slots, _ = lookup(request_ref, map_ref, owners, local_adapters)
    shape = (local_adapters, local_adapters)
    upto = hot(iota(shape, 1) <= iota(shape, 0))
    place = iota((local_adapters, capacity), 1)
    found = []
    for source in range(owners):
        slot = slots[:, source * rows : (source + 1) * rows]
        mine = iota((local_adapters, rows), 0) + me * local_adapters == slot
        counts = jnp.sum(jnp.where(mine, 1.0, 0.0), axis=1, keepdims=True)
        ends = column_sums(upto, counts).astype(jnp.int32)
        passed = jnp.sum(jnp.where(ends <= place, 1, 0), axis=0, keepdims=True)
        found.append(jnp.where(passed < local_adapters, passed, -1))
    size = capacity // GROUPS
    for group in range(GROUPS):
        span = slice(group * size, (group + 1) * size)
        pieces = []
        for k in range(owners):
            if group < GROUPS // 2:
                pieces.append(found[k][:, span])
                continue
            piece = found[0][:, span]
            for source in range(1, owners):
                here = lax.rem(me - k + owners, owners) == source
                piece = jnp.where(here, found[source][:, span], piece)
            pieces.append(piece)
        row = jnp.concatenate(pieces, axis=1)
        adapter_ref[:, group * owners * size : (group + 1) * owners * size] = jnp.broadcast_to(
            row, (8, owners * size)
        )
        bound_ref[2 * group] = jnp.min(jnp.where(row < 0, local_adapters, row))
        bound_ref[2 * group + 1] = jnp.max(row)


def plan(me, requests, slot_map, owners, local_adapters):
    rows = requests.shape[1] // owners
    vmem, smem = pl.BlockSpec(memory_space=pltpu.VMEM), pl.BlockSpec(memory_space=pltpu.SMEM)
    return pl.pallas_call(
        functools.partial(plan_kernel, owners, local_adapters, rows),
        in_specs=[smem, vmem, vmem],
        out_specs=[vmem, smem],
        out_shape=[
            jax.ShapeDtypeStruct((8, 2 * rows), jnp.int32),
            jax.ShapeDtypeStruct((2 * GROUPS,), jnp.int32),
        ],
        compiler_params=pltpu.CompilerParams(vmem_limit_bytes=VMEM_BYTES),
        cost_estimate=BRIEF,
        name="plan",
    )(me, requests, slot_map)


def base_kernel(me_ref, tokens_ref, weight_ref, near_ref, far_ref, give_ref, total_ref):
    total_ref[...] = jnp.dot(tokens_ref[...], weight_ref[...], preferred_element_type=jnp.float32)
    piece = near_ref.shape[1]
    for bit, out_ref in enumerate((near_ref, give_ref.at[0], far_ref, give_ref.at[1])):
        column = pl.multiple_of((me_ref[0] ^ bit) * piece, piece)
        out_ref[...] = total_ref[:, pl.ds(column, piece)]


def base_sum(tokens, weight):
    me = lax.axis_index("tensor").astype(jnp.int32).reshape(1)
    rows, columns = tokens.shape[0], weight.shape[1]
    vmem, smem = pl.BlockSpec(memory_space=pltpu.VMEM), pl.BlockSpec(memory_space=pltpu.SMEM)
    piece = jax.ShapeDtypeStruct((rows, columns // 4), jnp.float32)
    near, far, give = pl.pallas_call(
        base_kernel,
        in_specs=[smem, vmem, vmem],
        out_specs=[vmem] * 3,
        out_shape=[piece, piece, jax.ShapeDtypeStruct((2, *piece.shape), jnp.float32)],
        scratch_shapes=[pltpu.VMEM((rows, columns), jnp.float32)],
        compiler_params=pltpu.CompilerParams(vmem_limit_bytes=VMEM_BYTES),
        cost_estimate=BRIEF,
        name="base",
    )(me, tokens, weight)
    came = exchange(give, "tensor", 1)
    return near + came[0] + exchange(far + came[1], "tensor", 2)


def gather_rows(sent_refs, rows_ref, sems, owners):
    groups = GROUPS // 2
    size = rows_ref.shape[0] // groups
    share = size // owners
    copies = []
    for group in range(groups):
        for k in range(owners):
            if len(sent_refs) == 1:
                at = (groups * k + group) * share
                source = sent_refs[0].at[at : at + share]
            else:
                source = sent_refs[k].at[group * share : (group + 1) * share]
            target = rows_ref.at[group * size + k * share : group * size + (k + 1) * share]
            copies.append(pltpu.make_async_copy(source, target, sems.at[group * owners + k]))
    for copy in copies:
        copy.start()
    return copies


def add_blocks(part, rank, first, last, wait, bound_ref, adapter_ref, held_ref, rows_ref, total_ref):
    groups = GROUPS // 2
    size = rows_ref.shape[0] // groups
    wide = BLOCK * rank

    def block(step, carry):
        wait(step)
        start = step * BLOCK
        for group in range(groups):
            low, high = (bound_ref[2 * (part * groups + group) + k] for k in range(2))

            @pl.when((low < start + BLOCK) & (high >= start))
            def _():
                products = lax.dot_general(
                    held_ref[pl.ds(pl.multiple_of(step * wide, wide), wide), :],
                    rows_ref[group * size : (group + 1) * size, :],
                    NT,
                    preferred_element_type=jnp.float32,
                )
                at = (part * groups + group) * size
                total = total_ref[:, group * size : (group + 1) * size]
                for k in range(BLOCK):
                    chosen = adapter_ref[0:1, at : at + size] == start + k
                    total += jnp.where(chosen, products[k * rank : (k + 1) * rank], 0.0)
                total_ref[:, group * size : (group + 1) * size] = total

        return carry

    lax.fori_loop(first, last, block, 0)


def early_kernel(
    rank, owners, bound_ref, adapter_ref, down_ref, sent_ref,
    total_ref, held_ref, rows_ref, sems, held_sems,
):
    blocks = held_sems.shape[0]
    copies = gather_rows([sent_ref], rows_ref, sems, owners)
    fetches = start_copies(down_ref, held_ref, held_sems)
    total_ref[...] = jnp.zeros_like(total_ref)
    for copy in copies:
        copy.wait()

    def wait(step):
        at = pl.ds(pl.multiple_of(step * BLOCK * rank, BLOCK * rank), BLOCK * rank)
        pltpu.make_async_copy(down_ref.at[at], held_ref.at[at], held_sems.at[step]).wait()

    add_blocks(0, rank, 0, blocks, wait, bound_ref, adapter_ref, held_ref, rows_ref, total_ref)


def early_down(bounds, adapter_row, down_rows, sent, rank, owners):
    height, width = down_rows.shape
    slots = adapter_row.shape[1] // 2
    vmem, anywhere = pl.BlockSpec(memory_space=pltpu.VMEM), pl.BlockSpec(memory_space=pl.ANY)
    return pl.pallas_call(
        functools.partial(early_kernel, rank, owners),
        in_specs=[pl.BlockSpec(memory_space=pltpu.SMEM), vmem, anywhere, anywhere],
        out_specs=[vmem, vmem],
        out_shape=[
            jax.ShapeDtypeStruct((rank, slots), jnp.float32),
            pltpu.VMEM((height, width), jnp.bfloat16),
        ],
        scratch_shapes=[
            pltpu.VMEM((slots, width), jnp.bfloat16),
            pltpu.SemaphoreType.DMA((GROUPS // 2 * owners,)),
            pltpu.SemaphoreType.DMA((height // (BLOCK * rank),)),
        ],
        compiler_params=pltpu.CompilerParams(vmem_limit_bytes=VMEM_BYTES),
        cost_estimate=BRIEF,
        name="early_down",
    )(bounds, adapter_row, pltpu.with_memory_space_constraint(down_rows, pltpu.HBM), sent)


def late_kernel(rank, owners, *refs):
    bound_ref, side_ref, adapter_ref, held_ref, early_ref = refs[:5]
    sent_refs = refs[5 : 5 + owners]
    keep_ref, give_ref, rows_ref, total_ref, sems = refs[5 + owners :]
    copies = gather_rows(sent_refs, rows_ref, sems, owners)
    total_ref[...] = jnp.zeros_like(total_ref)
    groups = GROUPS // 2
    low, high = bound_ref[2 * groups], bound_ref[2 * groups + 1]
    for group in range(groups + 1, GROUPS):
        low = jnp.minimum(low, bound_ref[2 * group])
        high = jnp.maximum(high, bound_ref[2 * group + 1])
    first, last = lax.div(low, jnp.int32(BLOCK)), lax.div(high + BLOCK, jnp.int32(BLOCK))
    for copy in copies:
        copy.wait()
    add_blocks(
        1, rank, first, last, lambda step: None, bound_ref, adapter_ref, held_ref, rows_ref, total_ref
    )
    side = side_ref[0]
    one, two = early_ref[...], total_ref[...]
    keep_ref[...] = jnp.where(side == 0, one, two)
    give_ref[...] = jnp.where(side == 0, two, one)


def late_down(bounds, side, adapter_row, held, early, sent, rank, owners):
    width = held.shape[1]
    vmem, smem = pl.BlockSpec(memory_space=pltpu.VMEM), pl.BlockSpec(memory_space=pltpu.SMEM)
    return pl.pallas_call(
        functools.partial(late_kernel, rank, owners),
        in_specs=[smem, smem, vmem, vmem, vmem] + [pl.BlockSpec(memory_space=pl.ANY)] * owners,
        out_specs=[vmem, vmem],
        out_shape=[jax.ShapeDtypeStruct(early.shape, jnp.float32)] * 2,
        scratch_shapes=[
            pltpu.VMEM((early.shape[1], width), jnp.bfloat16),
            pltpu.VMEM(early.shape, jnp.float32),
            pltpu.SemaphoreType.DMA((GROUPS // 2 * owners,)),
        ],
        compiler_params=pltpu.CompilerParams(vmem_limit_bytes=VMEM_BYTES),
        cost_estimate=BRIEF,
        name="late_down",
    )(bounds, side, adapter_row, pltpu.with_memory_space_constraint(held, pltpu.VMEM), early, *sent)


def up_kernel(owners, rank, adapters, me_ref, side_ref, adapter_ref, up_ref, mine_ref, other_ref, out_ref):
    me, side = me_ref[0], side_ref[0]
    mine, other = mine_ref[...].astype(jnp.float32), other_ref[...].astype(jnp.float32)
    groups = GROUPS // 2
    size = mine.shape[1] // groups
    share = size // owners
    for group in range(GROUPS):
        part, inner = group // groups, group % groups
        span = slice(inner * size, (inner + 1) * size)
        low_rank = jnp.where(side == part, mine[:, span], other[:, span])
        chosen = adapter_ref[0:1, group * size : (group + 1) * size]
        spread = jnp.concatenate(
            [jnp.where(chosen == k, low_rank, 0.0).astype(jnp.bfloat16) for k in range(adapters)],
            axis=0,
        )
        delta = lax.dot_general(up_ref[...], spread, TN, preferred_element_type=jnp.float32)
        delta = delta.astype(jnp.bfloat16)
        for k in range(owners):
            source = k if part == 0 else lax.rem(me - k + owners, owners)
            out_ref[source, :, group * share : (group + 1) * share] = delta[:, k * share : (k + 1) * share]


def up(me, side, adapter_row, up_rows, mine, other, owners):
    rank, wide = mine.shape
    piece = up_rows.shape[1]
    adapters = up_rows.shape[0] // rank
    vmem, smem = pl.BlockSpec(memory_space=pltpu.VMEM), pl.BlockSpec(memory_space=pltpu.SMEM)
    return pl.pallas_call(
        functools.partial(up_kernel, owners, rank, adapters),
        in_specs=[smem, smem, vmem, vmem, vmem, vmem],
        out_shape=jax.ShapeDtypeStruct((owners, piece, 2 * wide // owners), jnp.bfloat16),
        compiler_params=pltpu.CompilerParams(vmem_limit_bytes=VMEM_BYTES),
        cost_estimate=BRIEF,
        name="up",
    )(me, side, adapter_row, up_rows, mine, other)


def tensor_sum(keep, give):
    keep = keep + exchange(give, "tensor", 1)
    keep = keep + exchange(keep, "tensor", 2)
    mine = keep.astype(jnp.bfloat16)
    return mine, exchange(mine, "tensor", 1)


def unpack_kernel(owners, place_ref, returned_ref, base_ref, out_ref, held_ref, sem):
    copy = pltpu.make_async_copy(base_ref, held_ref, sem)
    copy.start()
    rows, capacity = out_ref.shape[0], returned_ref.shape[2]
    total = jnp.zeros((returned_ref.shape[1], rows), jnp.float32)
    for owner in range(owners):
        selector = hot(iota((capacity, rows), 0) == place_ref[0:1, :] - owner * capacity)
        total += jnp.dot(returned_ref[owner], selector, preferred_element_type=jnp.float32)
    copy.wait()
    out_ref[...] = (held_ref[...] + ADAPTER_SCALE * total.T).astype(jnp.bfloat16)


def unpack(place, returned, base):
    vmem = pl.BlockSpec(memory_space=pltpu.VMEM)
    return pl.pallas_call(
        functools.partial(unpack_kernel, returned.shape[0]),
        in_specs=[vmem, vmem, pl.BlockSpec(memory_space=pl.ANY)],
        out_specs=vmem,
        out_shape=jax.ShapeDtypeStruct(base.shape, jnp.bfloat16),
        scratch_shapes=[pltpu.VMEM(base.shape, jnp.float32), pltpu.SemaphoreType.DMA],
        compiler_params=pltpu.CompilerParams(vmem_limit_bytes=VMEM_BYTES),
        cost_estimate=BRIEF,
        name="unpack",
    )(place, returned, base)


def exchange(array, axis, bit):
    size = lax.axis_size(axis)
    return lax.ppermute(array, axis, [(k, k ^ bit) for k in range(size)])


def swap(array):
    return lax.all_to_all(array, "replica", split_axis=0, concat_axis=0, tiled=True)


def body(tokens, value_weight, down_factor, up_factor, request_adapter, adapter_slot_map):
    row_count, quarter = tokens.shape
    owners = lax.axis_size("replica")
    local_adapters, _, rank = down_factor.shape
    half = row_count // owners
    me = lax.axis_index("replica").astype(jnp.int32).reshape(1)
    side = (lax.axis_index("tensor").astype(jnp.int32) % 2).reshape(1)
    requests = request_adapter.reshape(1, -1)
    slot_map = adapter_slot_map.reshape(1, -1)
    down_rows = jnp.swapaxes(down_factor, 1, 2).reshape(local_adapters * rank, quarter)
    up_rows = up_factor.reshape(local_adapters * rank, -1)

    first, over, place, branch = route(me, requests, slot_map, tokens, owners, local_adapters)

    def work(late, place, first, over, tokens, value_weight, down_rows, up_rows, requests, slot_map):
        arrived = swap(first.reshape(owners, half, quarter)).reshape(owners * half, quarter)
        base = base_sum(tokens, value_weight)
        adapter_row, bounds = plan(me, requests, slot_map, owners, local_adapters)
        adapter_row, base = lax.optimization_barrier((adapter_row, base))
        early, held = early_down(bounds, adapter_row, down_rows, arrived, rank, owners)
        keep, give = late_down(bounds, side, adapter_row, held, early, (over, *late), rank, owners)
        mine, other = tensor_sum(keep, give)
        delta = up(me, side, adapter_row, up_rows, mine, other, owners)
        return unpack(place, swap(delta), base)

    def to_one(owner):
        def send(place, first, over, tokens, *rest):
            late = tuple(
                lax.ppermute(over, "replica", [((owner - shift) % owners, owner)])
                for shift in range(1, owners)
            )
            return work(late, place, first, over, tokens, *rest)

        return send

    def to_all(place, first, over, tokens, *rest):
        spot = place[0]
        owner, late = spot // (2 * half), spot % (2 * half) - half
        index = jnp.where(late >= 0, owner * half + late, -1)
        packer = (jnp.arange(owners * half)[:, None] == index[None, :]).astype(jnp.bfloat16)
        outgoing = jnp.dot(packer, tokens, preferred_element_type=jnp.float32)
        outgoing = outgoing.astype(jnp.bfloat16).reshape(owners, half, quarter)
        came = lax.all_to_all(outgoing, "replica", split_axis=0, concat_axis=0, tiled=True)
        here = lax.axis_index("replica")
        late = tuple(
            lax.dynamic_index_in_dim(came, (here - shift) % owners, 0, keepdims=False)
            for shift in range(1, owners)
        )
        return work(late, place, first, over, tokens, *rest)

    return lax.switch(
        branch[0],
        [to_one(owner) for owner in range(owners)] + [to_all],
        place, first, over, tokens, value_weight, down_rows, up_rows, requests, slot_map,
    )


def solution(mesh):
    in_specs = (
        P(("parts", "replica"), "tensor"),
        P("tensor", None),
        P(("parts", "replica"), "tensor", None),
        P(("parts", "replica"), None, "tensor"),
        P("parts"),
        P("parts"),
    )
    out_specs = P(("parts", "replica"), "tensor")
    small = mesh.shape["replica"] <= MAX_OWNERS and mesh.shape["tensor"] == 4
    chosen = body if small else plain_body
    return jax.shard_map(chosen, mesh=mesh, in_specs=in_specs, out_specs=out_specs, check_vma=False)
```

```python
import functools

import jax
import jax.numpy as jnp
from jax import lax
from jax.experimental import pallas as pl
from jax.experimental.pallas import tpu as pltpu
from jax.sharding import PartitionSpec as P

ADAPTER_SCALE = 0.5
MAX_OWNERS = 8
COPIES = 8
GROUPS = 4
BLOCK = 4
BRIEF = pl.CostEstimate(flops=0, bytes_accessed=0, transcendentals=0)
VMEM_BYTES = 40 * 1024 * 1024
NT = (((1,), (1,)), ((), ()))
TN = (((0,), (0,)), ((), ()))


def plain_body(tokens, value_weight, down_factor, up_factor, request_adapter, adapter_slot_map):
    row_count, quarter = tokens.shape
    owners = lax.axis_size("replica")
    local_adapters = down_factor.shape[0]
    output_piece = up_factor.shape[2]
    capacity = 2 * row_count // owners
    my_index = lax.axis_index("replica")
    pool_slot = jnp.take(adapter_slot_map, request_adapter)
    owner_grid = (pool_slot // local_adapters).reshape(owners, row_count)
    local_grid = (pool_slot % local_adapters).reshape(owners, row_count)
    my_owner = lax.dynamic_slice_in_dim(owner_grid, my_index, 1, 0)[0]
    owner_hot = (my_owner[:, None] == jnp.arange(owners)[None, :]).astype(jnp.int32)
    my_rank = jnp.sum(jnp.cumsum(owner_hot, axis=0) * owner_hot, axis=1) - 1
    position = my_owner * capacity + my_rank
    packer = (jnp.arange(owners * capacity)[:, None] == position[None, :]).astype(jnp.bfloat16)
    outgoing = jnp.dot(packer, tokens, preferred_element_type=jnp.float32).astype(jnp.bfloat16)
    outgoing = outgoing.reshape(owners, capacity, quarter)
    partial_base = jnp.dot(tokens, value_weight, preferred_element_type=jnp.float32)
    arrived = lax.all_to_all(outgoing, "replica", split_axis=0, concat_axis=0, tiled=True)
    mine = (owner_grid == my_index).astype(jnp.int32)
    recv_rank = jnp.cumsum(mine, axis=1) - 1
    selector = (
        (recv_rank[:, None, :] == jnp.arange(capacity)[None, :, None]) & (mine[:, None, :] > 0)
    ).astype(jnp.int32)
    slot_local = jnp.sum(selector * local_grid[:, None, :], axis=2).reshape(owners * capacity)
    sort_order = jnp.argsort(slot_local, stable=True)
    inverse_order = jnp.argsort(sort_order)
    group_row_count = jnp.sum(
        (slot_local[:, None] == jnp.arange(local_adapters)[None, :]).astype(jnp.int32), axis=0
    )
    rows_by_adapter = jnp.take(arrived.reshape(owners * capacity, quarter), sort_order, axis=0)
    partial_rank = lax.ragged_dot(
        rows_by_adapter, down_factor, group_row_count, preferred_element_type=jnp.float32
    )
    rank_projected = lax.psum(partial_rank, "tensor").astype(jnp.bfloat16)
    sorted_delta = lax.ragged_dot(
        rank_projected, up_factor, group_row_count, preferred_element_type=jnp.float32
    ).astype(jnp.bfloat16)
    adapter_delta = jnp.take(sorted_delta, inverse_order, axis=0).reshape(
        owners, capacity, output_piece
    )
    returned = lax.all_to_all(adapter_delta, "replica", split_axis=0, concat_axis=0, tiled=True)
    adapter_delta_rows = jnp.einsum(
        "pr,po->ro",
        packer,
        returned.reshape(owners * capacity, output_piece),
        preferred_element_type=jnp.float32,
    )
    local_base_output = lax.psum_scatter(partial_base, "tensor", scatter_dimension=1, tiled=True)
    return (local_base_output + ADAPTER_SCALE * adapter_delta_rows).astype(jnp.bfloat16)


def iota(shape, dim):
    return lax.broadcasted_iota(jnp.int32, shape, dim)


def hot(mask):
    return jnp.where(mask, 1.0, 0.0).astype(jnp.bfloat16)


def lookup(request_ref, map_ref, owners, local_adapters):
    rows, adapters = request_ref.shape[1], map_ref.shape[1]
    slots = map_ref[...]
    which = iota((16, adapters), 0)
    owner = lax.div(slots, jnp.int32(local_adapters))
    table = jnp.where(which == 8, slots, jnp.where(which == owner, 1, 0))
    table = table.astype(jnp.float32).astype(jnp.bfloat16)
    one_hot = hot(iota((adapters, rows), 0) == request_ref[...])
    found = jnp.dot(table, one_hot, preferred_element_type=jnp.float32)
    return found[8:9].astype(jnp.int32), found[0:8]


def column_sums(table, counts):
    wide = jnp.broadcast_to(counts, (counts.shape[0], 128)).astype(jnp.bfloat16)
    return jnp.dot(table, wide, preferred_element_type=jnp.float32)[:, :1]


def start_copies(source_ref, target_ref, sems, offset=0):
    size = source_ref.shape[0] // sems.shape[0]
    copies = [
        pltpu.make_async_copy(
            source_ref.at[k * size : (k + 1) * size],
            target_ref.at[offset + k * size : offset + (k + 1) * size],
            sems.at[k],
        )
        for k in range(sems.shape[0])
    ]
    for copy in copies:
        copy.start()
    return copies


def route_kernel(
    owners, local_adapters, me_ref, request_ref, map_ref, tokens_ref,
    first_ref, over_ref, place_ref, branch_ref,
    request_held, map_held, rows_ref, packed_ref, sems, out_sems,
):
    small = [
        pltpu.make_async_copy(source, target, out_sems.at[k])
        for k, (source, target) in enumerate(((request_ref, request_held), (map_ref, map_held)))
    ]
    for copy in small:
        copy.start()
    rows, width = tokens_ref.shape
    capacity = 2 * rows // owners
    half = capacity // 2
    pool = map_ref.shape[1]
    copies = start_copies(tokens_ref, rows_ref, sems)
    me = me_ref[0]
    before = hot(iota((rows, rows), 0) < iota((rows, rows), 1))
    for copy in small:
        copy.wait()
    slots, marks = lookup(request_held, map_held, owners, local_adapters)
    most = jnp.zeros((8, 1), jnp.float32)
    slot = jnp.zeros((1, rows), jnp.int32)
    for source in range(owners):
        span = slice(source * rows, (source + 1) * rows)
        most = jnp.maximum(most, jnp.sum(marks[:, span], axis=1, keepdims=True))
        slot = jnp.where(me == source, slots[:, span], slot)
    over = jnp.where(most > half, 1, 0)
    branch = jnp.where(jnp.sum(over) <= 1, jnp.sum(over * iota((8, 1), 0)), owners)
    branch_ref[0] = branch
    mine = iota((pool, rows), 0) == slot
    one_hot = hot(mine)
    ranks = jnp.dot(one_hot, before, preferred_element_type=jnp.float32)
    counts = jnp.sum(jnp.where(mine, 1.0, 0.0), axis=1, keepdims=True)
    row, column = iota((pool, pool), 0), iota((pool, pool), 1)
    same = lax.div(row, jnp.int32(local_adapters)) == lax.div(column, jnp.int32(local_adapters))
    ranks += column_sums(hot(same & (column < row)), counts)
    rank = jnp.sum(jnp.where(mine, ranks, 0.0), axis=0, keepdims=True).astype(jnp.int32)
    owner = lax.div(slot, jnp.int32(local_adapters))
    place_ref[...] = jnp.broadcast_to(owner * capacity + rank, (8, rows))
    target = jnp.where(branch < owners, branch, me)
    late = jnp.where((owner == target) & (rank >= half), rank - half, -1)
    first = jnp.where(rank < half, owner * half + rank, -1)
    for copy in copies:
        copy.wait()
    sends = []
    for k in range(owners + 1):
        index = late if k == 0 else first - (k - 1) * half
        packer = hot(iota((half, rows), 0) == index)
        packed = jnp.dot(packer, rows_ref[...], preferred_element_type=jnp.float32)
        packed_ref[k * half : (k + 1) * half, :] = packed.astype(jnp.bfloat16)
        target_ref = over_ref if k == 0 else first_ref.at[(k - 1) * half : k * half]
        sends.append(
            pltpu.make_async_copy(packed_ref.at[k * half : (k + 1) * half], target_ref, out_sems.at[k])
        )
        sends[-1].start()
    for send in sends:
        send.wait()


def route(me, requests, slot_map, tokens, owners, local_adapters):
    rows, width = tokens.shape
    half = rows // owners
    vmem, smem = pl.BlockSpec(memory_space=pltpu.VMEM), pl.BlockSpec(memory_space=pltpu.SMEM)
    anywhere = pl.BlockSpec(memory_space=pl.ANY)
    return pl.pallas_call(
        functools.partial(route_kernel, owners, local_adapters),
        in_specs=[smem, anywhere, anywhere, anywhere],
        out_specs=[anywhere, anywhere, vmem, smem],
        out_shape=[
            pltpu.HBM((rows, width), jnp.bfloat16),
            pltpu.HBM((half, width), jnp.bfloat16),
            jax.ShapeDtypeStruct((8, rows), jnp.int32),
            jax.ShapeDtypeStruct((1,), jnp.int32),
        ],
        scratch_shapes=[
            pltpu.VMEM(requests.shape, jnp.int32),
            pltpu.VMEM(slot_map.shape, jnp.int32),
            pltpu.VMEM((rows, width), jnp.bfloat16),
            pltpu.VMEM((rows + half, width), jnp.bfloat16),
            pltpu.SemaphoreType.DMA((COPIES,)),
            pltpu.SemaphoreType.DMA((owners + 1,)),
        ],
        compiler_params=pltpu.CompilerParams(vmem_limit_bytes=VMEM_BYTES),
        name="route",
    )(me, requests, slot_map, tokens)


def plan_kernel(
    owners, local_adapters, rows, me_ref, request_ref, map_ref, adapter_ref, bound_ref
):
    me = me_ref[0]
    capacity = 2 * rows // owners
    slots, _ = lookup(request_ref, map_ref, owners, local_adapters)
    shape = (local_adapters, local_adapters)
    upto = hot(iota(shape, 1) <= iota(shape, 0))
    place = iota((local_adapters, capacity), 1)
    found = []
    for source in range(owners):
        slot = slots[:, source * rows : (source + 1) * rows]
        mine = iota((local_adapters, rows), 0) + me * local_adapters == slot
        counts = jnp.sum(jnp.where(mine, 1.0, 0.0), axis=1, keepdims=True)
        ends = column_sums(upto, counts).astype(jnp.int32)
        passed = jnp.sum(jnp.where(ends <= place, 1, 0), axis=0, keepdims=True)
        found.append(jnp.where(passed < local_adapters, passed, -1))
    size = capacity // GROUPS
    for group in range(GROUPS):
        span = slice(group * size, (group + 1) * size)
        pieces = []
        for k in range(owners):
            if group < GROUPS // 2:
                pieces.append(found[k][:, span])
                continue
            piece = found[0][:, span]
            for source in range(1, owners):
                here = lax.rem(me - k + owners, owners) == source
                piece = jnp.where(here, found[source][:, span], piece)
            pieces.append(piece)
        row = jnp.concatenate(pieces, axis=1)
        adapter_ref[:, group * owners * size : (group + 1) * owners * size] = jnp.broadcast_to(
            row, (8, owners * size)
        )
        bound_ref[2 * group] = jnp.min(jnp.where(row < 0, local_adapters, row))
        bound_ref[2 * group + 1] = jnp.max(row)


def plan(me, requests, slot_map, owners, local_adapters):
    rows = requests.shape[1] // owners
    vmem, smem = pl.BlockSpec(memory_space=pltpu.VMEM), pl.BlockSpec(memory_space=pltpu.SMEM)
    return pl.pallas_call(
        functools.partial(plan_kernel, owners, local_adapters, rows),
        in_specs=[smem, vmem, vmem],
        out_specs=[vmem, smem],
        out_shape=[
            jax.ShapeDtypeStruct((8, 2 * rows), jnp.int32),
            jax.ShapeDtypeStruct((2 * GROUPS,), jnp.int32),
        ],
        compiler_params=pltpu.CompilerParams(vmem_limit_bytes=VMEM_BYTES),
        cost_estimate=BRIEF,
        name="plan",
    )(me, requests, slot_map)


def base_kernel(me_ref, tokens_ref, weight_ref, near_ref, far_ref, give_ref, total_ref):
    total_ref[...] = jnp.dot(tokens_ref[...], weight_ref[...], preferred_element_type=jnp.float32)
    piece = near_ref.shape[1]
    for bit, out_ref in enumerate((near_ref, give_ref.at[0], far_ref, give_ref.at[1])):
        column = pl.multiple_of((me_ref[0] ^ bit) * piece, piece)
        out_ref[...] = total_ref[:, pl.ds(column, piece)]


def base_sum(tokens, weight):
    me = lax.axis_index("tensor").astype(jnp.int32).reshape(1)
    rows, columns = tokens.shape[0], weight.shape[1]
    vmem, smem = pl.BlockSpec(memory_space=pltpu.VMEM), pl.BlockSpec(memory_space=pltpu.SMEM)
    piece = jax.ShapeDtypeStruct((rows, columns // 4), jnp.float32)
    near, far, give = pl.pallas_call(
        base_kernel,
        in_specs=[smem, vmem, vmem],
        out_specs=[vmem] * 3,
        out_shape=[piece, piece, jax.ShapeDtypeStruct((2, *piece.shape), jnp.float32)],
        scratch_shapes=[pltpu.VMEM((rows, columns), jnp.float32)],
        compiler_params=pltpu.CompilerParams(vmem_limit_bytes=VMEM_BYTES),
        cost_estimate=BRIEF,
        name="base",
    )(me, tokens, weight)
    came = exchange(give, "tensor", 1)
    return near + came[0] + exchange(far + came[1], "tensor", 2)


def gather_rows(sent_refs, rows_ref, sems, owners):
    groups = GROUPS // 2
    size = rows_ref.shape[0] // groups
    share = size // owners
    copies = []
    for group in range(groups):
        for k in range(owners):
            if len(sent_refs) == 1:
                at = (groups * k + group) * share
                source = sent_refs[0].at[at : at + share]
            else:
                source = sent_refs[k].at[group * share : (group + 1) * share]
            target = rows_ref.at[group * size + k * share : group * size + (k + 1) * share]
            copies.append(pltpu.make_async_copy(source, target, sems.at[group * owners + k]))
    for copy in copies:
        copy.start()
    return copies


def add_blocks(part, rank, first, last, wait, bound_ref, adapter_ref, held_ref, rows_ref, total_ref):
    groups = GROUPS // 2
    size = rows_ref.shape[0] // groups
    wide = BLOCK * rank

    def block(step, carry):
        wait(step)
        start = step * BLOCK
        for group in range(groups):
            low, high = (bound_ref[2 * (part * groups + group) + k] for k in range(2))

            @pl.when((low < start + BLOCK) & (high >= start))
            def _():
                products = lax.dot_general(
                    held_ref[pl.ds(pl.multiple_of(step * wide, wide), wide), :],
                    rows_ref[group * size : (group + 1) * size, :],
                    NT,
                    preferred_element_type=jnp.float32,
                )
                at = (part * groups + group) * size
                total = total_ref[:, group * size : (group + 1) * size]
                for k in range(BLOCK):
                    chosen = adapter_ref[0:1, at : at + size] == start + k
                    total += jnp.where(chosen, products[k * rank : (k + 1) * rank], 0.0)
                total_ref[:, group * size : (group + 1) * size] = total

        return carry

    lax.fori_loop(first, last, block, 0)


def early_kernel(
    rank, owners, bound_ref, adapter_ref, down_ref, sent_ref,
    total_ref, held_ref, rows_ref, sems, held_sems,
):
    blocks = held_sems.shape[0]
    copies = gather_rows([sent_ref], rows_ref, sems, owners)
    fetches = start_copies(down_ref, held_ref, held_sems)
    total_ref[...] = jnp.zeros_like(total_ref)
    for copy in copies:
        copy.wait()

    def wait(step):
        at = pl.ds(pl.multiple_of(step * BLOCK * rank, BLOCK * rank), BLOCK * rank)
        pltpu.make_async_copy(down_ref.at[at], held_ref.at[at], held_sems.at[step]).wait()

    add_blocks(0, rank, 0, blocks, wait, bound_ref, adapter_ref, held_ref, rows_ref, total_ref)


def early_down(bounds, adapter_row, down_rows, sent, rank, owners):
    height, width = down_rows.shape
    slots = adapter_row.shape[1] // 2
    vmem, anywhere = pl.BlockSpec(memory_space=pltpu.VMEM), pl.BlockSpec(memory_space=pl.ANY)
    return pl.pallas_call(
        functools.partial(early_kernel, rank, owners),
        in_specs=[pl.BlockSpec(memory_space=pltpu.SMEM), vmem, anywhere, anywhere],
        out_specs=[vmem, vmem],
        out_shape=[
            jax.ShapeDtypeStruct((rank, slots), jnp.float32),
            pltpu.VMEM((height, width), jnp.bfloat16),
        ],
        scratch_shapes=[
            pltpu.VMEM((slots, width), jnp.bfloat16),
            pltpu.SemaphoreType.DMA((GROUPS // 2 * owners,)),
            pltpu.SemaphoreType.DMA((height // (BLOCK * rank),)),
        ],
        compiler_params=pltpu.CompilerParams(vmem_limit_bytes=VMEM_BYTES),
        cost_estimate=BRIEF,
        name="early_down",
    )(bounds, adapter_row, pltpu.with_memory_space_constraint(down_rows, pltpu.HBM), sent)


def late_kernel(rank, owners, *refs):
    bound_ref, side_ref, adapter_ref, held_ref, early_ref = refs[:5]
    sent_refs = refs[5 : 5 + owners]
    keep_ref, give_ref, rows_ref, total_ref, sems = refs[5 + owners :]
    copies = gather_rows(sent_refs, rows_ref, sems, owners)
    groups = GROUPS // 2
    size = rows_ref.shape[0] // groups
    wide = BLOCK * rank
    pool = held_ref.shape[0] // rank
    total_ref[...] = jnp.zeros_like(total_ref)
    for group in range(groups):
        low, high = (bound_ref[2 * (groups + group) + k] for k in range(2))
        span = slice(group * size, (group + 1) * size)
        at = (groups + group) * size
        for copy in copies[group * owners : (group + 1) * owners]:
            copy.wait()

        def block(step, carry):
            fresh = low + step * BLOCK
            start = jnp.minimum(fresh, pool - BLOCK)
            products = lax.dot_general(
                held_ref[pl.ds(pl.multiple_of(start * rank, rank), wide), :],
                rows_ref[span, :],
                NT,
                preferred_element_type=jnp.float32,
            )
            adapter = adapter_ref[0:1, at : at + size]
            adapter = jnp.where(adapter < fresh, -1, adapter - start)
            total = total_ref[:, span]
            for k in range(BLOCK):
                total += jnp.where(adapter == k, products[k * rank : (k + 1) * rank], 0.0)
            total_ref[:, span] = total
            return carry

        lax.fori_loop(0, lax.div(high - low + BLOCK, jnp.int32(BLOCK)), block, 0)
    side = side_ref[0]
    one, two = early_ref[...], total_ref[...]
    keep_ref[...] = jnp.where(side == 0, one, two)
    give_ref[...] = jnp.where(side == 0, two, one)


def late_down(bounds, side, adapter_row, held, early, sent, rank, owners):
    width = held.shape[1]
    vmem, smem = pl.BlockSpec(memory_space=pltpu.VMEM), pl.BlockSpec(memory_space=pltpu.SMEM)
    return pl.pallas_call(
        functools.partial(late_kernel, rank, owners),
        in_specs=[smem, smem, vmem, vmem, vmem] + [pl.BlockSpec(memory_space=pl.ANY)] * owners,
        out_specs=[vmem, vmem],
        out_shape=[jax.ShapeDtypeStruct(early.shape, jnp.float32)] * 2,
        scratch_shapes=[
            pltpu.VMEM((early.shape[1], width), jnp.bfloat16),
            pltpu.VMEM(early.shape, jnp.float32),
            pltpu.SemaphoreType.DMA((GROUPS // 2 * owners,)),
        ],
        compiler_params=pltpu.CompilerParams(vmem_limit_bytes=VMEM_BYTES),
        cost_estimate=BRIEF,
        name="late_down",
    )(bounds, side, adapter_row, pltpu.with_memory_space_constraint(held, pltpu.VMEM), early, *sent)


def up_kernel(owners, rank, adapters, me_ref, side_ref, adapter_ref, up_ref, mine_ref, other_ref, *refs):
    out_refs, held_ref = refs[:-1], refs[-1]
    me, side = me_ref[0], side_ref[0]
    mine, other = mine_ref[...].astype(jnp.float32), other_ref[...].astype(jnp.float32)
    groups = GROUPS // 2
    size = mine.shape[1] // groups
    share = size // owners
    for group in range(GROUPS):
        part, inner = group // groups, group % groups
        span = slice(inner * size, (inner + 1) * size)
        low_rank = jnp.where(side == part, mine[:, span], other[:, span])
        chosen = adapter_ref[0:1, group * size : (group + 1) * size]
        spread = jnp.concatenate(
            [jnp.where(chosen == k, low_rank, 0.0).astype(jnp.bfloat16) for k in range(adapters)],
            axis=0,
        )
        delta = lax.dot_general(up_ref[...], spread, TN, preferred_element_type=jnp.float32)
        delta = delta.astype(jnp.bfloat16)
        for k in range(owners):
            source = (k if part == 0 else lax.rem(me - k + owners, owners)) ^ me
            held_ref[source, :, group * share : (group + 1) * share] = delta[:, k * share : (k + 1) * share]
    for bit, out_ref in enumerate(out_refs):
        out_ref[...] = held_ref[bit]


def up(me, side, adapter_row, up_rows, mine, other, owners):
    rank, wide = mine.shape
    piece = up_rows.shape[1]
    adapters = up_rows.shape[0] // rank
    vmem, smem = pl.BlockSpec(memory_space=pltpu.VMEM), pl.BlockSpec(memory_space=pltpu.SMEM)
    return pl.pallas_call(
        functools.partial(up_kernel, owners, rank, adapters),
        in_specs=[smem, smem, vmem, vmem, vmem, vmem],
        out_shape=[jax.ShapeDtypeStruct((piece, 2 * wide // owners), jnp.bfloat16)] * owners,
        scratch_shapes=[pltpu.VMEM((owners, piece, 2 * wide // owners), jnp.bfloat16)],
        compiler_params=pltpu.CompilerParams(vmem_limit_bytes=VMEM_BYTES),
        cost_estimate=BRIEF,
        name="up",
    )(me, side, adapter_row, up_rows, mine, other)


def tensor_sum(keep, give):
    keep = keep + exchange(give, "tensor", 1)
    keep = keep + exchange(keep, "tensor", 2)
    mine = keep.astype(jnp.bfloat16)
    return mine, exchange(mine, "tensor", 1)


def unpack_kernel(owners, me_ref, place_ref, *refs):
    returned_refs, base_ref, out_ref, held_ref, sem = refs[:owners], *refs[owners:]
    copy = pltpu.make_async_copy(base_ref, held_ref, sem)
    copy.start()
    rows = out_ref.shape[0]
    features, capacity = returned_refs[0].shape
    total = jnp.zeros((features, rows), jnp.float32)
    for bit in range(owners):
        spot = place_ref[0:1, :] - (me_ref[0] ^ bit) * capacity
        selector = hot(iota((capacity, rows), 0) == spot)
        total += jnp.dot(returned_refs[bit][...], selector, preferred_element_type=jnp.float32)
    copy.wait()
    out_ref[...] = (held_ref[...] + ADAPTER_SCALE * total.T).astype(jnp.bfloat16)


def unpack(me, place, returned, base):
    vmem, smem = pl.BlockSpec(memory_space=pltpu.VMEM), pl.BlockSpec(memory_space=pltpu.SMEM)
    return pl.pallas_call(
        functools.partial(unpack_kernel, len(returned)),
        in_specs=[smem, vmem] + [vmem] * len(returned) + [pl.BlockSpec(memory_space=pl.ANY)],
        out_specs=vmem,
        out_shape=pltpu.HBM(base.shape, jnp.bfloat16),
        scratch_shapes=[pltpu.VMEM(base.shape, jnp.float32), pltpu.SemaphoreType.DMA],
        compiler_params=pltpu.CompilerParams(vmem_limit_bytes=VMEM_BYTES),
        cost_estimate=BRIEF,
        name="unpack",
    )(me, place, *returned, base)


def exchange(array, axis, bit):
    size = lax.axis_size(axis)
    return lax.ppermute(array, axis, [(k, k ^ bit) for k in range(size)])


def swap(array):
    return lax.all_to_all(array, "replica", split_axis=0, concat_axis=0, tiled=True)


def body(tokens, value_weight, down_factor, up_factor, request_adapter, adapter_slot_map):
    row_count, quarter = tokens.shape
    owners = lax.axis_size("replica")
    local_adapters, _, rank = down_factor.shape
    half = row_count // owners
    me = lax.axis_index("replica").astype(jnp.int32).reshape(1)
    side = (lax.axis_index("tensor").astype(jnp.int32) % 2).reshape(1)
    requests = request_adapter.reshape(1, -1)
    slot_map = adapter_slot_map.reshape(1, -1)
    down_rows = jnp.swapaxes(down_factor, 1, 2).reshape(local_adapters * rank, quarter)
    up_rows = up_factor.reshape(local_adapters * rank, -1)

    first, over, place, branch = route(me, requests, slot_map, tokens, owners, local_adapters)

    def work(late, place, first, over, tokens, value_weight, down_rows, up_rows, requests, slot_map):
        arrived = swap(first.reshape(owners, half, quarter)).reshape(owners * half, quarter)
        base = base_sum(tokens, value_weight)
        adapter_row, bounds = plan(me, requests, slot_map, owners, local_adapters)
        adapter_row, base = lax.optimization_barrier((adapter_row, base))
        early, held = early_down(bounds, adapter_row, down_rows, arrived, rank, owners)
        keep, give = late_down(bounds, side, adapter_row, held, early, (over, *late), rank, owners)
        mine, other = tensor_sum(keep, give)
        delta = up(me, side, adapter_row, up_rows, mine, other, owners)
        returned = [delta[0]] + [exchange(delta[bit], "replica", bit) for bit in range(1, owners)]
        return unpack(me, place, returned, base)

    def to_one(owner):
        def send(place, first, over, tokens, *rest):
            late = tuple(
                lax.ppermute(over, "replica", [((owner - shift) % owners, owner)])
                for shift in range(1, owners)
            )
            return work(late, place, first, over, tokens, *rest)

        return send

    def to_all(place, first, over, tokens, *rest):
        spot = place[0]
        owner, late = spot // (2 * half), spot % (2 * half) - half
        index = jnp.where(late >= 0, owner * half + late, -1)
        packer = (jnp.arange(owners * half)[:, None] == index[None, :]).astype(jnp.bfloat16)
        outgoing = jnp.dot(packer, tokens, preferred_element_type=jnp.float32)
        outgoing = outgoing.astype(jnp.bfloat16).reshape(owners, half, quarter)
        came = lax.all_to_all(outgoing, "replica", split_axis=0, concat_axis=0, tiled=True)
        here = lax.axis_index("replica")
        late = tuple(
            lax.dynamic_index_in_dim(came, (here - shift) % owners, 0, keepdims=False)
            for shift in range(1, owners)
        )
        return work(late, place, first, over, tokens, *rest)

    return lax.switch(
        branch[0],
        [to_one(owner) for owner in range(owners)] + [to_all],
        place, first, over, tokens, value_weight, down_rows, up_rows, requests, slot_map,
    )


def solution(mesh):
    in_specs = (
        P(("parts", "replica"), "tensor"),
        P("tensor", None),
        P(("parts", "replica"), "tensor", None),
        P(("parts", "replica"), None, "tensor"),
        P("parts"),
        P("parts"),
    )
    out_specs = P(("parts", "replica"), "tensor")
    small = mesh.shape["replica"] <= MAX_OWNERS and mesh.shape["tensor"] == 4
    chosen = body if small else plain_body
    return jax.shard_map(chosen, mesh=mesh, in_specs=in_specs, out_specs=out_specs, check_vma=False)
```

```python
import functools

import jax
import jax.numpy as jnp
from jax import lax
from jax.experimental import pallas as pl
from jax.experimental.pallas import tpu as pltpu
from jax.sharding import PartitionSpec as P

ADAPTER_SCALE = 0.5
COPIES = 8
GROUPS = 4
BLOCK = 4
BRIEF = pl.CostEstimate(flops=0, bytes_accessed=0, transcendentals=0)
VMEM_BYTES = 40 * 1024 * 1024
NT = (((1,), (1,)), ((), ()))
TN = (((0,), (0,)), ((), ()))


def plain_body(tokens, value_weight, down_factor, up_factor, request_adapter, adapter_slot_map):
    row_count, quarter = tokens.shape
    owners = lax.axis_size("replica")
    local_adapters = down_factor.shape[0]
    output_piece = up_factor.shape[2]
    capacity = 2 * row_count // owners
    my_index = lax.axis_index("replica")
    pool_slot = jnp.take(adapter_slot_map, request_adapter)
    owner_grid = (pool_slot // local_adapters).reshape(owners, row_count)
    local_grid = (pool_slot % local_adapters).reshape(owners, row_count)
    my_owner = lax.dynamic_slice_in_dim(owner_grid, my_index, 1, 0)[0]
    owner_hot = (my_owner[:, None] == jnp.arange(owners)[None, :]).astype(jnp.int32)
    my_rank = jnp.sum(jnp.cumsum(owner_hot, axis=0) * owner_hot, axis=1) - 1
    position = my_owner * capacity + my_rank
    packer = (jnp.arange(owners * capacity)[:, None] == position[None, :]).astype(jnp.bfloat16)
    outgoing = jnp.dot(packer, tokens, preferred_element_type=jnp.float32).astype(jnp.bfloat16)
    outgoing = outgoing.reshape(owners, capacity, quarter)
    partial_base = jnp.dot(tokens, value_weight, preferred_element_type=jnp.float32)
    arrived = lax.all_to_all(outgoing, "replica", split_axis=0, concat_axis=0, tiled=True)
    mine = (owner_grid == my_index).astype(jnp.int32)
    recv_rank = jnp.cumsum(mine, axis=1) - 1
    selector = (
        (recv_rank[:, None, :] == jnp.arange(capacity)[None, :, None]) & (mine[:, None, :] > 0)
    ).astype(jnp.int32)
    slot_local = jnp.sum(selector * local_grid[:, None, :], axis=2).reshape(owners * capacity)
    sort_order = jnp.argsort(slot_local, stable=True)
    inverse_order = jnp.argsort(sort_order)
    group_row_count = jnp.sum(
        (slot_local[:, None] == jnp.arange(local_adapters)[None, :]).astype(jnp.int32), axis=0
    )
    rows_by_adapter = jnp.take(arrived.reshape(owners * capacity, quarter), sort_order, axis=0)
    partial_rank = lax.ragged_dot(
        rows_by_adapter, down_factor, group_row_count, preferred_element_type=jnp.float32
    )
    rank_projected = lax.psum(partial_rank, "tensor").astype(jnp.bfloat16)
    sorted_delta = lax.ragged_dot(
        rank_projected, up_factor, group_row_count, preferred_element_type=jnp.float32
    ).astype(jnp.bfloat16)
    adapter_delta = jnp.take(sorted_delta, inverse_order, axis=0).reshape(
        owners, capacity, output_piece
    )
    returned = lax.all_to_all(adapter_delta, "replica", split_axis=0, concat_axis=0, tiled=True)
    adapter_delta_rows = jnp.einsum(
        "pr,po->ro",
        packer,
        returned.reshape(owners * capacity, output_piece),
        preferred_element_type=jnp.float32,
    )
    local_base_output = lax.psum_scatter(partial_base, "tensor", scatter_dimension=1, tiled=True)
    return (local_base_output + ADAPTER_SCALE * adapter_delta_rows).astype(jnp.bfloat16)


def iota(shape, dim):
    return lax.broadcasted_iota(jnp.int32, shape, dim)


def hot(mask):
    return jnp.where(mask, 1.0, 0.0).astype(jnp.bfloat16)


def lookup(request_ref, map_ref, owners, local_adapters):
    rows, adapters = request_ref.shape[1], map_ref.shape[1]
    slots = map_ref[...]
    which = iota((16, adapters), 0)
    owner = lax.div(slots, jnp.int32(local_adapters))
    table = jnp.where(which == 8, slots, jnp.where(which == owner, 1, 0))
    table = table.astype(jnp.float32).astype(jnp.bfloat16)
    one_hot = hot(iota((adapters, rows), 0) == request_ref[...])
    found = jnp.dot(table, one_hot, preferred_element_type=jnp.float32)
    return found[8:9].astype(jnp.int32), found[0:8]


def column_sums(table, counts):
    wide = jnp.broadcast_to(counts, (counts.shape[0], 128)).astype(jnp.bfloat16)
    return jnp.dot(table, wide, preferred_element_type=jnp.float32)[:, :1]


def start_copies(source_ref, target_ref, sems, offset=0):
    size = source_ref.shape[0] // sems.shape[0]
    copies = [
        pltpu.make_async_copy(
            source_ref.at[k * size : (k + 1) * size],
            target_ref.at[offset + k * size : offset + (k + 1) * size],
            sems.at[k],
        )
        for k in range(sems.shape[0])
    ]
    for copy in copies:
        copy.start()
    return copies


def route_kernel(
    owners, local_adapters, me_ref, request_ref, map_ref, tokens_ref,
    first_ref, over_ref, place_ref, branch_ref,
    request_held, map_held, rows_ref, packed_ref, sems, out_sems,
):
    small = [
        pltpu.make_async_copy(source, target, out_sems.at[k])
        for k, (source, target) in enumerate(((request_ref, request_held), (map_ref, map_held)))
    ]
    for copy in small:
        copy.start()
    rows, width = tokens_ref.shape
    capacity = 2 * rows // owners
    half = capacity // 2
    pool = map_ref.shape[1]
    copies = start_copies(tokens_ref, rows_ref, sems)
    me = me_ref[0]
    before = hot(iota((rows, rows), 0) < iota((rows, rows), 1))
    for copy in small:
        copy.wait()
    slots, marks = lookup(request_held, map_held, owners, local_adapters)
    most = jnp.zeros((8, 1), jnp.float32)
    slot = jnp.zeros((1, rows), jnp.int32)
    for source in range(owners):
        span = slice(source * rows, (source + 1) * rows)
        most = jnp.maximum(most, jnp.sum(marks[:, span], axis=1, keepdims=True))
        slot = jnp.where(me == source, slots[:, span], slot)
    over = jnp.where(most > half, 1, 0)
    branch = jnp.where(jnp.sum(over) <= 1, jnp.sum(over * iota((8, 1), 0)), owners)
    branch_ref[0] = branch
    mine = iota((pool, rows), 0) == slot
    one_hot = hot(mine)
    ranks = jnp.dot(one_hot, before, preferred_element_type=jnp.float32)
    counts = jnp.sum(jnp.where(mine, 1.0, 0.0), axis=1, keepdims=True)
    row, column = iota((pool, pool), 0), iota((pool, pool), 1)
    same = lax.div(row, jnp.int32(local_adapters)) == lax.div(column, jnp.int32(local_adapters))
    ranks += column_sums(hot(same & (column < row)), counts)
    rank = jnp.sum(jnp.where(mine, ranks, 0.0), axis=0, keepdims=True).astype(jnp.int32)
    owner = lax.div(slot, jnp.int32(local_adapters))
    place_ref[...] = jnp.broadcast_to(owner * capacity + rank, (8, rows))
    target = jnp.where(branch < owners, branch, me)
    late = jnp.where((owner == target) & (rank >= half), rank - half, -1)
    first = jnp.where(rank < half, owner * half + rank, -1)
    for copy in copies:
        copy.wait()
    sends = []
    for k in range(owners + 1):
        index = late if k == 0 else first - (k - 1) * half
        packer = hot(iota((half, rows), 0) == index)
        packed = jnp.dot(packer, rows_ref[...], preferred_element_type=jnp.float32)
        packed_ref[k * half : (k + 1) * half, :] = packed.astype(jnp.bfloat16)
        target_ref = over_ref if k == 0 else first_ref.at[(k - 1) * half : k * half]
        sends.append(
            pltpu.make_async_copy(packed_ref.at[k * half : (k + 1) * half], target_ref, out_sems.at[k])
        )
        sends[-1].start()
    for send in sends:
        send.wait()


def route(me, requests, slot_map, tokens, owners, local_adapters):
    rows, width = tokens.shape
    half = rows // owners
    vmem, smem = pl.BlockSpec(memory_space=pltpu.VMEM), pl.BlockSpec(memory_space=pltpu.SMEM)
    anywhere = pl.BlockSpec(memory_space=pl.ANY)
    return pl.pallas_call(
        functools.partial(route_kernel, owners, local_adapters),
        in_specs=[smem, anywhere, anywhere, anywhere],
        out_specs=[anywhere, anywhere, vmem, smem],
        out_shape=[
            pltpu.HBM((rows, width), jnp.bfloat16),
            pltpu.HBM((half, width), jnp.bfloat16),
            jax.ShapeDtypeStruct((8, rows), jnp.int32),
            jax.ShapeDtypeStruct((1,), jnp.int32),
        ],
        scratch_shapes=[
            pltpu.VMEM(requests.shape, jnp.int32),
            pltpu.VMEM(slot_map.shape, jnp.int32),
            pltpu.VMEM((rows, width), jnp.bfloat16),
            pltpu.VMEM((rows + half, width), jnp.bfloat16),
            pltpu.SemaphoreType.DMA((COPIES,)),
            pltpu.SemaphoreType.DMA((owners + 1,)),
        ],
        compiler_params=pltpu.CompilerParams(vmem_limit_bytes=VMEM_BYTES),
        name="route",
    )(me, requests, slot_map, tokens)


def plan_kernel(
    owners, local_adapters, rows, me_ref, request_ref, map_ref, adapter_ref, bound_ref
):
    me = me_ref[0]
    capacity = 2 * rows // owners
    slots, _ = lookup(request_ref, map_ref, owners, local_adapters)
    shape = (local_adapters, local_adapters)
    upto = hot(iota(shape, 1) <= iota(shape, 0))
    place = iota((local_adapters, capacity), 1)
    found = []
    for source in range(owners):
        slot = slots[:, source * rows : (source + 1) * rows]
        mine = iota((local_adapters, rows), 0) + me * local_adapters == slot
        counts = jnp.sum(jnp.where(mine, 1.0, 0.0), axis=1, keepdims=True)
        ends = column_sums(upto, counts).astype(jnp.int32)
        passed = jnp.sum(jnp.where(ends <= place, 1, 0), axis=0, keepdims=True)
        found.append(jnp.where(passed < local_adapters, passed, -1))
    size = capacity // GROUPS
    for group in range(GROUPS):
        span = slice(group * size, (group + 1) * size)
        pieces = []
        for k in range(owners):
            if group < GROUPS // 2:
                pieces.append(found[k][:, span])
                continue
            piece = found[0][:, span]
            for source in range(1, owners):
                here = lax.rem(me - k + owners, owners) == source
                piece = jnp.where(here, found[source][:, span], piece)
            pieces.append(piece)
        row = jnp.concatenate(pieces, axis=1)
        adapter_ref[:, group * owners * size : (group + 1) * owners * size] = jnp.broadcast_to(
            row, (8, owners * size)
        )
        bound_ref[2 * group] = jnp.min(jnp.where(row < 0, local_adapters, row))
        bound_ref[2 * group + 1] = jnp.max(row)


def plan(me, requests, slot_map, owners, local_adapters):
    rows = requests.shape[1] // owners
    vmem, smem = pl.BlockSpec(memory_space=pltpu.VMEM), pl.BlockSpec(memory_space=pltpu.SMEM)
    return pl.pallas_call(
        functools.partial(plan_kernel, owners, local_adapters, rows),
        in_specs=[smem, vmem, vmem],
        out_specs=[vmem, smem],
        out_shape=[
            jax.ShapeDtypeStruct((8, 2 * rows), jnp.int32),
            jax.ShapeDtypeStruct((2 * GROUPS,), jnp.int32),
        ],
        compiler_params=pltpu.CompilerParams(vmem_limit_bytes=VMEM_BYTES),
        cost_estimate=BRIEF,
        name="plan",
    )(me, requests, slot_map)


def base_kernel(me_ref, tokens_ref, weight_ref, near_ref, far_ref, give_ref, total_ref):
    total_ref[...] = jnp.dot(tokens_ref[...], weight_ref[...], preferred_element_type=jnp.float32)
    piece = near_ref.shape[1]
    for bit, out_ref in enumerate((near_ref, give_ref.at[0], far_ref, give_ref.at[1])):
        column = pl.multiple_of((me_ref[0] ^ bit) * piece, piece)
        out_ref[...] = total_ref[:, pl.ds(column, piece)]


def base_sum(tokens, weight):
    me = lax.axis_index("tensor").astype(jnp.int32).reshape(1)
    rows, columns = tokens.shape[0], weight.shape[1]
    vmem, smem = pl.BlockSpec(memory_space=pltpu.VMEM), pl.BlockSpec(memory_space=pltpu.SMEM)
    piece = jax.ShapeDtypeStruct((rows, columns // 4), jnp.float32)
    near, far, give = pl.pallas_call(
        base_kernel,
        in_specs=[smem, vmem, vmem],
        out_specs=[vmem] * 3,
        out_shape=[piece, piece, jax.ShapeDtypeStruct((2, *piece.shape), jnp.float32)],
        scratch_shapes=[pltpu.VMEM((rows, columns), jnp.float32)],
        compiler_params=pltpu.CompilerParams(vmem_limit_bytes=VMEM_BYTES),
        cost_estimate=BRIEF,
        name="base",
    )(me, tokens, weight)
    came = exchange(give, "tensor", 1)
    return near + came[0] + exchange(far + came[1], "tensor", 2)


def gather_rows(sent_refs, rows_ref, sems, owners):
    groups = GROUPS // 2
    size = rows_ref.shape[0] // groups
    share = size // owners
    copies = []
    for group in range(groups):
        for k in range(owners):
            if len(sent_refs) == 1:
                at = (groups * k + group) * share
                source = sent_refs[0].at[at : at + share]
            else:
                source = sent_refs[k].at[group * share : (group + 1) * share]
            target = rows_ref.at[group * size + k * share : group * size + (k + 1) * share]
            copies.append(pltpu.make_async_copy(source, target, sems.at[group * owners + k]))
    for copy in copies:
        copy.start()
    return copies


def add_blocks(part, rank, first, last, wait, bound_ref, adapter_ref, held_ref, rows_ref, total_ref):
    groups = GROUPS // 2
    size = rows_ref.shape[0] // groups
    wide = BLOCK * rank

    def block(step, carry):
        wait(step)
        start = step * BLOCK
        for group in range(groups):
            low, high = (bound_ref[2 * (part * groups + group) + k] for k in range(2))

            @pl.when((low < start + BLOCK) & (high >= start))
            def _():
                products = lax.dot_general(
                    held_ref[pl.ds(pl.multiple_of(step * wide, wide), wide), :],
                    rows_ref[group * size : (group + 1) * size, :],
                    NT,
                    preferred_element_type=jnp.float32,
                )
                at = (part * groups + group) * size
                total = total_ref[:, group * size : (group + 1) * size]
                for k in range(BLOCK):
                    chosen = adapter_ref[0:1, at : at + size] == start + k
                    total += jnp.where(chosen, products[k * rank : (k + 1) * rank], 0.0)
                total_ref[:, group * size : (group + 1) * size] = total

        return carry

    lax.fori_loop(first, last, block, 0)


def early_kernel(
    rank, owners, bound_ref, adapter_ref, down_ref, sent_ref,
    total_ref, held_ref, rows_ref, sems, held_sems,
):
    blocks = held_sems.shape[0]
    copies = gather_rows([sent_ref], rows_ref, sems, owners)
    fetches = start_copies(down_ref, held_ref, held_sems)
    total_ref[...] = jnp.zeros_like(total_ref)
    for copy in copies:
        copy.wait()

    def wait(step):
        at = pl.ds(pl.multiple_of(step * BLOCK * rank, BLOCK * rank), BLOCK * rank)
        pltpu.make_async_copy(down_ref.at[at], held_ref.at[at], held_sems.at[step]).wait()

    add_blocks(0, rank, 0, blocks, wait, bound_ref, adapter_ref, held_ref, rows_ref, total_ref)


def early_down(bounds, adapter_row, down_rows, sent, rank, owners):
    height, width = down_rows.shape
    slots = adapter_row.shape[1] // 2
    vmem, anywhere = pl.BlockSpec(memory_space=pltpu.VMEM), pl.BlockSpec(memory_space=pl.ANY)
    return pl.pallas_call(
        functools.partial(early_kernel, rank, owners),
        in_specs=[pl.BlockSpec(memory_space=pltpu.SMEM), vmem, anywhere, anywhere],
        out_specs=[vmem, vmem],
        out_shape=[
            jax.ShapeDtypeStruct((rank, slots), jnp.float32),
            pltpu.VMEM((height, width), jnp.bfloat16),
        ],
        scratch_shapes=[
            pltpu.VMEM((slots, width), jnp.bfloat16),
            pltpu.SemaphoreType.DMA((GROUPS // 2 * owners,)),
            pltpu.SemaphoreType.DMA((height // (BLOCK * rank),)),
        ],
        compiler_params=pltpu.CompilerParams(vmem_limit_bytes=VMEM_BYTES),
        cost_estimate=BRIEF,
        name="early_down",
    )(bounds, adapter_row, pltpu.with_memory_space_constraint(down_rows, pltpu.HBM), sent)


def late_kernel(rank, owners, *refs):
    bound_ref, side_ref, adapter_ref, held_ref, early_ref = refs[:5]
    sent_refs = refs[5 : 5 + owners]
    keep_ref, give_ref, rows_ref, total_ref, sems = refs[5 + owners :]
    copies = gather_rows(sent_refs, rows_ref, sems, owners)
    groups = GROUPS // 2
    size = rows_ref.shape[0] // groups
    wide = BLOCK * rank
    pool = held_ref.shape[0] // rank
    total_ref[...] = jnp.zeros_like(total_ref)
    for group in range(groups):
        low, high = (bound_ref[2 * (groups + group) + k] for k in range(2))
        span = slice(group * size, (group + 1) * size)
        at = (groups + group) * size
        for copy in copies[group * owners : (group + 1) * owners]:
            copy.wait()

        def block(step, carry):
            fresh = low + step * BLOCK
            start = jnp.minimum(fresh, pool - BLOCK)
            products = lax.dot_general(
                held_ref[pl.ds(pl.multiple_of(start * rank, rank), wide), :],
                rows_ref[span, :],
                NT,
                preferred_element_type=jnp.float32,
            )
            adapter = adapter_ref[0:1, at : at + size]
            adapter = jnp.where(adapter < fresh, -1, adapter - start)
            total = total_ref[:, span]
            for k in range(BLOCK):
                total += jnp.where(adapter == k, products[k * rank : (k + 1) * rank], 0.0)
            total_ref[:, span] = total
            return carry

        lax.fori_loop(0, lax.div(high - low + BLOCK, jnp.int32(BLOCK)), block, 0)
    side = side_ref[0]
    one, two = early_ref[...], total_ref[...]
    keep_ref[...] = jnp.where(side == 0, one, two)
    give_ref[...] = jnp.where(side == 0, two, one)


def late_down(bounds, side, adapter_row, held, early, sent, rank, owners):
    width = held.shape[1]
    vmem, smem = pl.BlockSpec(memory_space=pltpu.VMEM), pl.BlockSpec(memory_space=pltpu.SMEM)
    return pl.pallas_call(
        functools.partial(late_kernel, rank, owners),
        in_specs=[smem, smem, vmem, vmem, vmem] + [pl.BlockSpec(memory_space=pl.ANY)] * owners,
        out_specs=[vmem, vmem],
        out_shape=[jax.ShapeDtypeStruct(early.shape, jnp.float32)] * 2,
        scratch_shapes=[
            pltpu.VMEM((early.shape[1], width), jnp.bfloat16),
            pltpu.VMEM(early.shape, jnp.float32),
            pltpu.SemaphoreType.DMA((GROUPS // 2 * owners,)),
        ],
        compiler_params=pltpu.CompilerParams(vmem_limit_bytes=VMEM_BYTES),
        cost_estimate=BRIEF,
        name="late_down",
    )(bounds, side, adapter_row, pltpu.with_memory_space_constraint(held, pltpu.VMEM), early, *sent)


def up_kernel(owners, rank, adapters, me_ref, side_ref, adapter_ref, up_ref, mine_ref, other_ref, *refs):
    out_refs, held_ref = refs[:-1], refs[-1]
    me, side = me_ref[0], side_ref[0]
    mine, other = mine_ref[...].astype(jnp.float32), other_ref[...].astype(jnp.float32)
    groups = GROUPS // 2
    size = mine.shape[1] // groups
    share = size // owners
    for group in range(GROUPS):
        part, inner = group // groups, group % groups
        span = slice(inner * size, (inner + 1) * size)
        low_rank = jnp.where(side == part, mine[:, span], other[:, span])
        chosen = adapter_ref[0:1, group * size : (group + 1) * size]
        spread = jnp.concatenate(
            [jnp.where(chosen == k, low_rank, 0.0).astype(jnp.bfloat16) for k in range(adapters)],
            axis=0,
        )
        delta = lax.dot_general(up_ref[...], spread, TN, preferred_element_type=jnp.float32)
        delta = delta.astype(jnp.bfloat16)
        for k in range(owners):
            source = (k if part == 0 else lax.rem(me - k + owners, owners)) ^ me
            held_ref[source, :, group * share : (group + 1) * share] = delta[:, k * share : (k + 1) * share]
    for bit, out_ref in enumerate(out_refs):
        out_ref[...] = held_ref[bit]


def up(me, side, adapter_row, up_rows, mine, other, owners):
    rank, wide = mine.shape
    piece = up_rows.shape[1]
    adapters = up_rows.shape[0] // rank
    vmem, smem = pl.BlockSpec(memory_space=pltpu.VMEM), pl.BlockSpec(memory_space=pltpu.SMEM)
    return pl.pallas_call(
        functools.partial(up_kernel, owners, rank, adapters),
        in_specs=[smem, smem, vmem, vmem, vmem, vmem],
        out_shape=[jax.ShapeDtypeStruct((piece, 2 * wide // owners), jnp.bfloat16)] * owners,
        scratch_shapes=[pltpu.VMEM((owners, piece, 2 * wide // owners), jnp.bfloat16)],
        compiler_params=pltpu.CompilerParams(vmem_limit_bytes=VMEM_BYTES),
        cost_estimate=BRIEF,
        name="up",
    )(me, side, adapter_row, up_rows, mine, other)


def tensor_sum(keep, give):
    keep = keep + exchange(give, "tensor", 1)
    keep = keep + exchange(keep, "tensor", 2)
    mine = keep.astype(jnp.bfloat16)
    return mine, exchange(mine, "tensor", 1)


def return_order(owners):
    return [*range(2, owners), 1, 0]


def unpack_kernel(owners, me_ref, place_ref, *refs):
    returned_refs, base_ref, out_ref, held_ref, sem = refs[:owners], *refs[owners:]
    copy = pltpu.make_async_copy(base_ref, held_ref, sem)
    copy.start()
    rows = out_ref.shape[0]
    features, capacity = returned_refs[0].shape
    total = jnp.zeros((features, rows), jnp.float32)
    for k, bit in enumerate(return_order(owners)):
        spot = place_ref[0:1, :] - (me_ref[0] ^ bit) * capacity
        selector = hot(iota((capacity, rows), 0) == spot)
        total += jnp.dot(returned_refs[k][...], selector, preferred_element_type=jnp.float32)
    copy.wait()
    out_ref[...] = (held_ref[...] + ADAPTER_SCALE * total.T).astype(jnp.bfloat16)


def unpack(me, place, returned, base):
    vmem, smem = pl.BlockSpec(memory_space=pltpu.VMEM), pl.BlockSpec(memory_space=pltpu.SMEM)
    return pl.pallas_call(
        functools.partial(unpack_kernel, len(returned)),
        in_specs=[smem, vmem] + [vmem] * len(returned) + [pl.BlockSpec(memory_space=pl.ANY)],
        out_specs=vmem,
        out_shape=pltpu.HBM(base.shape, jnp.bfloat16),
        scratch_shapes=[pltpu.VMEM(base.shape, jnp.float32), pltpu.SemaphoreType.DMA],
        compiler_params=pltpu.CompilerParams(vmem_limit_bytes=VMEM_BYTES),
        cost_estimate=BRIEF,
        name="unpack",
    )(me, place, *returned, base)


def exchange(array, axis, bit):
    size = lax.axis_size(axis)
    return lax.ppermute(array, axis, [(k, k ^ bit) for k in range(size)])


def swap(array):
    return lax.all_to_all(array, "replica", split_axis=0, concat_axis=0, tiled=True)


def body(tokens, value_weight, down_factor, up_factor, request_adapter, adapter_slot_map):
    row_count, quarter = tokens.shape
    owners = lax.axis_size("replica")
    local_adapters, _, rank = down_factor.shape
    half = row_count // owners
    me = lax.axis_index("replica").astype(jnp.int32).reshape(1)
    side = (lax.axis_index("tensor").astype(jnp.int32) % 2).reshape(1)
    requests = request_adapter.reshape(1, -1)
    slot_map = adapter_slot_map.reshape(1, -1)
    down_rows = jnp.swapaxes(down_factor, 1, 2).reshape(local_adapters * rank, quarter)
    up_rows = up_factor.reshape(local_adapters * rank, -1)

    first, over, place, branch = route(me, requests, slot_map, tokens, owners, local_adapters)

    def work(late, place, first, over, tokens, value_weight, down_rows, up_rows, requests, slot_map):
        arrived = swap(first.reshape(owners, half, quarter)).reshape(owners * half, quarter)
        base = base_sum(tokens, value_weight)
        adapter_row, bounds = plan(me, requests, slot_map, owners, local_adapters)
        adapter_row, base = lax.optimization_barrier((adapter_row, base))
        early, held = early_down(bounds, adapter_row, down_rows, arrived, rank, owners)
        keep, give = late_down(bounds, side, adapter_row, held, early, (over, *late), rank, owners)
        mine, other = tensor_sum(keep, give)
        delta = up(me, side, adapter_row, up_rows, mine, other, owners)
        returned = [exchange(delta[bit], "replica", bit) for bit in return_order(owners)[:-1]]
        returned.append(delta[0])
        return unpack(me, place, returned, base)

    def to_one(owner):
        def send(place, first, over, tokens, *rest):
            late = tuple(
                lax.ppermute(over, "replica", [((owner - shift) % owners, owner)])
                for shift in range(1, owners)
            )
            return work(late, place, first, over, tokens, *rest)

        return send

    def to_all(place, first, over, tokens, *rest):
        spot = place[0]
        owner, late = spot // (2 * half), spot % (2 * half) - half
        index = jnp.where(late >= 0, owner * half + late, -1)
        packer = (jnp.arange(owners * half)[:, None] == index[None, :]).astype(jnp.bfloat16)
        outgoing = jnp.dot(packer, tokens, preferred_element_type=jnp.float32)
        outgoing = outgoing.astype(jnp.bfloat16).reshape(owners, half, quarter)
        came = lax.all_to_all(outgoing, "replica", split_axis=0, concat_axis=0, tiled=True)
        here = lax.axis_index("replica")
        late = tuple(
            lax.dynamic_index_in_dim(came, (here - shift) % owners, 0, keepdims=False)
            for shift in range(1, owners)
        )
        return work(late, place, first, over, tokens, *rest)

    return lax.switch(
        branch[0],
        [to_one(owner) for owner in range(owners)] + [to_all],
        place, first, over, tokens, value_weight, down_rows, up_rows, requests, slot_map,
    )


def solution(mesh):
    in_specs = (
        P(("parts", "replica"), "tensor"),
        P("tensor", None),
        P(("parts", "replica"), "tensor", None),
        P(("parts", "replica"), None, "tensor"),
        P("parts"),
        P("parts"),
    )
    out_specs = P(("parts", "replica"), "tensor")
    small = mesh.shape["replica"] in (2, 4, 8) and mesh.shape["tensor"] == 4
    chosen = body if small else plain_body
    return jax.shard_map(chosen, mesh=mesh, in_specs=in_specs, out_specs=out_specs, check_vma=False)
```

```python
import functools

import jax
import jax.numpy as jnp
from jax import lax
from jax.experimental import pallas as pl
from jax.experimental.pallas import tpu as pltpu
from jax.sharding import PartitionSpec as P

ADAPTER_SCALE = 0.5
COPIES = 8
GROUPS = 4
BLOCK = 4
BRIEF = pl.CostEstimate(flops=0, bytes_accessed=0, transcendentals=0)
VMEM_BYTES = 40 * 1024 * 1024
NT = (((1,), (1,)), ((), ()))
TN = (((0,), (0,)), ((), ()))


def plain_body(tokens, value_weight, down_factor, up_factor, request_adapter, adapter_slot_map):
    row_count, quarter = tokens.shape
    owners = lax.axis_size("replica")
    local_adapters = down_factor.shape[0]
    output_piece = up_factor.shape[2]
    capacity = 2 * row_count // owners
    my_index = lax.axis_index("replica")
    pool_slot = jnp.take(adapter_slot_map, request_adapter)
    owner_grid = (pool_slot // local_adapters).reshape(owners, row_count)
    local_grid = (pool_slot % local_adapters).reshape(owners, row_count)
    my_owner = lax.dynamic_slice_in_dim(owner_grid, my_index, 1, 0)[0]
    owner_hot = (my_owner[:, None] == jnp.arange(owners)[None, :]).astype(jnp.int32)
    my_rank = jnp.sum(jnp.cumsum(owner_hot, axis=0) * owner_hot, axis=1) - 1
    position = my_owner * capacity + my_rank
    packer = (jnp.arange(owners * capacity)[:, None] == position[None, :]).astype(jnp.bfloat16)
    outgoing = jnp.dot(packer, tokens, preferred_element_type=jnp.float32).astype(jnp.bfloat16)
    outgoing = outgoing.reshape(owners, capacity, quarter)
    partial_base = jnp.dot(tokens, value_weight, preferred_element_type=jnp.float32)
    arrived = lax.all_to_all(outgoing, "replica", split_axis=0, concat_axis=0, tiled=True)
    mine = (owner_grid == my_index).astype(jnp.int32)
    recv_rank = jnp.cumsum(mine, axis=1) - 1
    selector = (
        (recv_rank[:, None, :] == jnp.arange(capacity)[None, :, None]) & (mine[:, None, :] > 0)
    ).astype(jnp.int32)
    slot_local = jnp.sum(selector * local_grid[:, None, :], axis=2).reshape(owners * capacity)
    sort_order = jnp.argsort(slot_local, stable=True)
    inverse_order = jnp.argsort(sort_order)
    group_row_count = jnp.sum(
        (slot_local[:, None] == jnp.arange(local_adapters)[None, :]).astype(jnp.int32), axis=0
    )
    rows_by_adapter = jnp.take(arrived.reshape(owners * capacity, quarter), sort_order, axis=0)
    partial_rank = lax.ragged_dot(
        rows_by_adapter, down_factor, group_row_count, preferred_element_type=jnp.float32
    )
    rank_projected = lax.psum(partial_rank, "tensor").astype(jnp.bfloat16)
    sorted_delta = lax.ragged_dot(
        rank_projected, up_factor, group_row_count, preferred_element_type=jnp.float32
    ).astype(jnp.bfloat16)
    adapter_delta = jnp.take(sorted_delta, inverse_order, axis=0).reshape(
        owners, capacity, output_piece
    )
    returned = lax.all_to_all(adapter_delta, "replica", split_axis=0, concat_axis=0, tiled=True)
    adapter_delta_rows = jnp.einsum(
        "pr,po->ro",
        packer,
        returned.reshape(owners * capacity, output_piece),
        preferred_element_type=jnp.float32,
    )
    local_base_output = lax.psum_scatter(partial_base, "tensor", scatter_dimension=1, tiled=True)
    return (local_base_output + ADAPTER_SCALE * adapter_delta_rows).astype(jnp.bfloat16)


def iota(shape, dim):
    return lax.broadcasted_iota(jnp.int32, shape, dim)


def hot(mask):
    return jnp.where(mask, 1.0, 0.0).astype(jnp.bfloat16)


def lookup(request_ref, map_ref, owners, local_adapters):
    rows, adapters = request_ref.shape[1], map_ref.shape[1]
    slots = map_ref[...]
    which = iota((16, adapters), 0)
    owner = lax.div(slots, jnp.int32(local_adapters))
    table = jnp.where(which == 8, slots, jnp.where(which == owner, 1, 0))
    table = table.astype(jnp.float32).astype(jnp.bfloat16)
    one_hot = hot(iota((adapters, rows), 0) == request_ref[...])
    found = jnp.dot(table, one_hot, preferred_element_type=jnp.float32)
    return found[8:9].astype(jnp.int32), found[0:8]


def column_sums(table, counts):
    wide = jnp.broadcast_to(counts, (counts.shape[0], 128)).astype(jnp.bfloat16)
    return jnp.dot(table, wide, preferred_element_type=jnp.float32)[:, :1]


def start_copies(source_ref, target_ref, sems, offset=0):
    size = source_ref.shape[0] // sems.shape[0]
    copies = [
        pltpu.make_async_copy(
            source_ref.at[k * size : (k + 1) * size],
            target_ref.at[offset + k * size : offset + (k + 1) * size],
            sems.at[k],
        )
        for k in range(sems.shape[0])
    ]
    for copy in copies:
        copy.start()
    return copies


def route_kernel(
    owners, local_adapters, me_ref, request_ref, map_ref, tokens_ref,
    first_ref, over_ref, place_ref, branch_ref,
    request_held, map_held, rows_ref, packed_ref, sems, out_sems,
):
    small = [
        pltpu.make_async_copy(source, target, out_sems.at[k])
        for k, (source, target) in enumerate(((request_ref, request_held), (map_ref, map_held)))
    ]
    for copy in small:
        copy.start()
    rows, width = tokens_ref.shape
    capacity = 2 * rows // owners
    half = capacity // 2
    pool = map_ref.shape[1]
    copies = start_copies(tokens_ref, rows_ref, sems)
    me = me_ref[0]
    before = hot(iota((rows, rows), 0) < iota((rows, rows), 1))
    for copy in small:
        copy.wait()
    slots, marks = lookup(request_held, map_held, owners, local_adapters)
    most = jnp.zeros((8, 1), jnp.float32)
    slot = jnp.zeros((1, rows), jnp.int32)
    for source in range(owners):
        span = slice(source * rows, (source + 1) * rows)
        most = jnp.maximum(most, jnp.sum(marks[:, span], axis=1, keepdims=True))
        slot = jnp.where(me == source, slots[:, span], slot)
    over = jnp.where(most > half, 1, 0)
    branch = jnp.where(jnp.sum(over) <= 1, jnp.sum(over * iota((8, 1), 0)), owners)
    branch_ref[0] = branch
    mine = iota((pool, rows), 0) == slot
    one_hot = hot(mine)
    ranks = jnp.dot(one_hot, before, preferred_element_type=jnp.float32)
    counts = jnp.sum(jnp.where(mine, 1.0, 0.0), axis=1, keepdims=True)
    row, column = iota((pool, pool), 0), iota((pool, pool), 1)
    same = lax.div(row, jnp.int32(local_adapters)) == lax.div(column, jnp.int32(local_adapters))
    ranks += column_sums(hot(same & (column > row)), counts)
    rank = jnp.sum(jnp.where(mine, ranks, 0.0), axis=0, keepdims=True).astype(jnp.int32)
    owner = lax.div(slot, jnp.int32(local_adapters))
    place_ref[...] = jnp.broadcast_to(owner * capacity + rank, (8, rows))
    target = jnp.where(branch < owners, branch, me)
    late = jnp.where((owner == target) & (rank >= half), rank - half, -1)
    first = jnp.where(rank < half, owner * half + rank, -1)
    for copy in copies:
        copy.wait()
    sends = []
    for k in range(owners + 1):
        index = late if k == 0 else first - (k - 1) * half
        packer = hot(iota((half, rows), 0) == index)
        packed = jnp.dot(packer, rows_ref[...], preferred_element_type=jnp.float32)
        packed_ref[k * half : (k + 1) * half, :] = packed.astype(jnp.bfloat16)
        target_ref = over_ref if k == 0 else first_ref.at[(k - 1) * half : k * half]
        sends.append(
            pltpu.make_async_copy(packed_ref.at[k * half : (k + 1) * half], target_ref, out_sems.at[k])
        )
        sends[-1].start()
    for send in sends:
        send.wait()


def route(me, requests, slot_map, tokens, owners, local_adapters):
    rows, width = tokens.shape
    half = rows // owners
    vmem, smem = pl.BlockSpec(memory_space=pltpu.VMEM), pl.BlockSpec(memory_space=pltpu.SMEM)
    anywhere = pl.BlockSpec(memory_space=pl.ANY)
    return pl.pallas_call(
        functools.partial(route_kernel, owners, local_adapters),
        in_specs=[smem, anywhere, anywhere, anywhere],
        out_specs=[anywhere, anywhere, vmem, smem],
        out_shape=[
            pltpu.HBM((rows, width), jnp.bfloat16),
            pltpu.HBM((half, width), jnp.bfloat16),
            jax.ShapeDtypeStruct((8, rows), jnp.int32),
            jax.ShapeDtypeStruct((1,), jnp.int32),
        ],
        scratch_shapes=[
            pltpu.VMEM(requests.shape, jnp.int32),
            pltpu.VMEM(slot_map.shape, jnp.int32),
            pltpu.VMEM((rows, width), jnp.bfloat16),
            pltpu.VMEM((rows + half, width), jnp.bfloat16),
            pltpu.SemaphoreType.DMA((COPIES,)),
            pltpu.SemaphoreType.DMA((owners + 1,)),
        ],
        compiler_params=pltpu.CompilerParams(vmem_limit_bytes=VMEM_BYTES),
        name="route",
    )(me, requests, slot_map, tokens)


def plan_kernel(
    owners, local_adapters, rows, me_ref, request_ref, map_ref, adapter_ref, bound_ref
):
    me = me_ref[0]
    capacity = 2 * rows // owners
    slots, _ = lookup(request_ref, map_ref, owners, local_adapters)
    shape = (local_adapters, local_adapters)
    onward = hot(iota(shape, 1) >= iota(shape, 0))
    place = iota((local_adapters, capacity), 1)
    found = []
    for source in range(owners):
        slot = slots[:, source * rows : (source + 1) * rows]
        mine = iota((local_adapters, rows), 0) + me * local_adapters == slot
        counts = jnp.sum(jnp.where(mine, 1.0, 0.0), axis=1, keepdims=True)
        ends = column_sums(onward, counts).astype(jnp.int32)
        passed = jnp.sum(jnp.where(ends <= place, 1, 0), axis=0, keepdims=True)
        found.append(local_adapters - 1 - passed)
    size = capacity // GROUPS
    for group in range(GROUPS):
        span = slice(group * size, (group + 1) * size)
        pieces = []
        for k in range(owners):
            if group < GROUPS // 2:
                pieces.append(found[k][:, span])
                continue
            piece = found[0][:, span]
            for source in range(1, owners):
                here = lax.rem(me - k + owners, owners) == source
                piece = jnp.where(here, found[source][:, span], piece)
            pieces.append(piece)
        row = jnp.concatenate(pieces, axis=1)
        adapter_ref[:, group * owners * size : (group + 1) * owners * size] = jnp.broadcast_to(
            row, (8, owners * size)
        )
        bound_ref[2 * group] = jnp.min(jnp.where(row < 0, local_adapters, row))
        bound_ref[2 * group + 1] = jnp.max(row)


def plan(me, requests, slot_map, owners, local_adapters):
    rows = requests.shape[1] // owners
    vmem, smem = pl.BlockSpec(memory_space=pltpu.VMEM), pl.BlockSpec(memory_space=pltpu.SMEM)
    return pl.pallas_call(
        functools.partial(plan_kernel, owners, local_adapters, rows),
        in_specs=[smem, vmem, vmem],
        out_specs=[vmem, smem],
        out_shape=[
            jax.ShapeDtypeStruct((8, 2 * rows), jnp.int32),
            jax.ShapeDtypeStruct((2 * GROUPS,), jnp.int32),
        ],
        compiler_params=pltpu.CompilerParams(vmem_limit_bytes=VMEM_BYTES),
        cost_estimate=BRIEF,
        name="plan",
    )(me, requests, slot_map)


def base_kernel(me_ref, tokens_ref, weight_ref, near_ref, far_ref, give_ref, total_ref):
    total_ref[...] = jnp.dot(tokens_ref[...], weight_ref[...], preferred_element_type=jnp.float32)
    piece = near_ref.shape[1]
    for bit, out_ref in enumerate((near_ref, give_ref.at[0], far_ref, give_ref.at[1])):
        column = pl.multiple_of((me_ref[0] ^ bit) * piece, piece)
        out_ref[...] = total_ref[:, pl.ds(column, piece)]


def base_sum(tokens, weight):
    me = lax.axis_index("tensor").astype(jnp.int32).reshape(1)
    rows, columns = tokens.shape[0], weight.shape[1]
    vmem, smem = pl.BlockSpec(memory_space=pltpu.VMEM), pl.BlockSpec(memory_space=pltpu.SMEM)
    piece = jax.ShapeDtypeStruct((rows, columns // 4), jnp.float32)
    near, far, give = pl.pallas_call(
        base_kernel,
        in_specs=[smem, vmem, vmem],
        out_specs=[vmem] * 3,
        out_shape=[piece, piece, jax.ShapeDtypeStruct((2, *piece.shape), jnp.float32)],
        scratch_shapes=[pltpu.VMEM((rows, columns), jnp.float32)],
        compiler_params=pltpu.CompilerParams(vmem_limit_bytes=VMEM_BYTES),
        cost_estimate=BRIEF,
        name="base",
    )(me, tokens, weight)
    came = exchange(give, "tensor", 1)
    return near + came[0] + exchange(far + came[1], "tensor", 2)


def gather_rows(sent_refs, rows_ref, sems, owners):
    groups = GROUPS // 2
    size = rows_ref.shape[0] // groups
    share = size // owners
    copies = []
    for group in range(groups):
        for k in range(owners):
            if len(sent_refs) == 1:
                at = (groups * k + group) * share
                source = sent_refs[0].at[at : at + share]
            else:
                source = sent_refs[k].at[group * share : (group + 1) * share]
            target = rows_ref.at[group * size + k * share : group * size + (k + 1) * share]
            copies.append(pltpu.make_async_copy(source, target, sems.at[group * owners + k]))
    for copy in copies:
        copy.start()
    return copies


def add_blocks(part, rank, first, last, wait, bound_ref, adapter_ref, held_ref, rows_ref, total_ref):
    groups = GROUPS // 2
    size = rows_ref.shape[0] // groups
    wide = BLOCK * rank

    def block(step, carry):
        wait(step)
        start = step * BLOCK
        for group in range(groups):
            low, high = (bound_ref[2 * (part * groups + group) + k] for k in range(2))

            @pl.when((low < start + BLOCK) & (high >= start))
            def _():
                products = lax.dot_general(
                    held_ref[pl.ds(pl.multiple_of(step * wide, wide), wide), :],
                    rows_ref[group * size : (group + 1) * size, :],
                    NT,
                    preferred_element_type=jnp.float32,
                )
                at = (part * groups + group) * size
                total = total_ref[:, group * size : (group + 1) * size]
                for k in range(BLOCK):
                    chosen = adapter_ref[0:1, at : at + size] == start + k
                    total += jnp.where(chosen, products[k * rank : (k + 1) * rank], 0.0)
                total_ref[:, group * size : (group + 1) * size] = total

        return carry

    lax.fori_loop(first, last, block, 0)


def early_kernel(
    rank, owners, bound_ref, adapter_ref, down_ref, sent_ref,
    total_ref, held_ref, rows_ref, sems, held_sems,
):
    blocks = held_sems.shape[0]
    copies = gather_rows([sent_ref], rows_ref, sems, owners)
    fetches = start_copies(down_ref, held_ref, held_sems)
    total_ref[...] = jnp.zeros_like(total_ref)
    for copy in copies:
        copy.wait()

    def wait(step):
        at = pl.ds(pl.multiple_of(step * BLOCK * rank, BLOCK * rank), BLOCK * rank)
        pltpu.make_async_copy(down_ref.at[at], held_ref.at[at], held_sems.at[step]).wait()

    add_blocks(0, rank, 0, blocks, wait, bound_ref, adapter_ref, held_ref, rows_ref, total_ref)


def early_down(bounds, adapter_row, down_rows, sent, rank, owners):
    height, width = down_rows.shape
    slots = adapter_row.shape[1] // 2
    vmem, anywhere = pl.BlockSpec(memory_space=pltpu.VMEM), pl.BlockSpec(memory_space=pl.ANY)
    return pl.pallas_call(
        functools.partial(early_kernel, rank, owners),
        in_specs=[pl.BlockSpec(memory_space=pltpu.SMEM), vmem, anywhere, anywhere],
        out_specs=[vmem, vmem],
        out_shape=[
            jax.ShapeDtypeStruct((rank, slots), jnp.float32),
            pltpu.VMEM((height, width), jnp.bfloat16),
        ],
        scratch_shapes=[
            pltpu.VMEM((slots, width), jnp.bfloat16),
            pltpu.SemaphoreType.DMA((GROUPS // 2 * owners,)),
            pltpu.SemaphoreType.DMA((height // (BLOCK * rank),)),
        ],
        compiler_params=pltpu.CompilerParams(vmem_limit_bytes=VMEM_BYTES),
        cost_estimate=BRIEF,
        name="early_down",
    )(bounds, adapter_row, pltpu.with_memory_space_constraint(down_rows, pltpu.HBM), sent)


def late_kernel(rank, owners, *refs):
    bound_ref, side_ref, adapter_ref, held_ref, early_ref = refs[:5]
    sent_refs = refs[5 : 5 + owners]
    keep_ref, give_ref, rows_ref, total_ref, sems = refs[5 + owners :]
    copies = gather_rows(sent_refs, rows_ref, sems, owners)
    groups = GROUPS // 2
    size = rows_ref.shape[0] // groups
    wide = BLOCK * rank
    pool = held_ref.shape[0] // rank
    total_ref[...] = jnp.zeros_like(total_ref)
    for group in range(groups):
        low, high = (bound_ref[2 * (groups + group) + k] for k in range(2))
        span = slice(group * size, (group + 1) * size)
        at = (groups + group) * size
        for copy in copies[group * owners : (group + 1) * owners]:
            copy.wait()

        def block(step, carry):
            fresh = low + step * BLOCK
            start = jnp.minimum(fresh, pool - BLOCK)
            products = lax.dot_general(
                held_ref[pl.ds(pl.multiple_of(start * rank, rank), wide), :],
                rows_ref[span, :],
                NT,
                preferred_element_type=jnp.float32,
            )
            adapter = adapter_ref[0:1, at : at + size]
            adapter = jnp.where(adapter < fresh, -1, adapter - start)
            total = total_ref[:, span]
            for k in range(BLOCK):
                total += jnp.where(adapter == k, products[k * rank : (k + 1) * rank], 0.0)
            total_ref[:, span] = total
            return carry

        lax.fori_loop(0, lax.div(high - low + BLOCK, jnp.int32(BLOCK)), block, 0)
    side = side_ref[0]
    one, two = early_ref[...], total_ref[...]
    keep_ref[...] = jnp.where(side == 0, one, two)
    give_ref[...] = jnp.where(side == 0, two, one)


def late_down(bounds, side, adapter_row, held, early, sent, rank, owners):
    width = held.shape[1]
    vmem, smem = pl.BlockSpec(memory_space=pltpu.VMEM), pl.BlockSpec(memory_space=pltpu.SMEM)
    return pl.pallas_call(
        functools.partial(late_kernel, rank, owners),
        in_specs=[smem, smem, vmem, vmem, vmem] + [pl.BlockSpec(memory_space=pl.ANY)] * owners,
        out_specs=[vmem, vmem],
        out_shape=[jax.ShapeDtypeStruct(early.shape, jnp.float32)] * 2,
        scratch_shapes=[
            pltpu.VMEM((early.shape[1], width), jnp.bfloat16),
            pltpu.VMEM(early.shape, jnp.float32),
            pltpu.SemaphoreType.DMA((GROUPS // 2 * owners,)),
        ],
        compiler_params=pltpu.CompilerParams(vmem_limit_bytes=VMEM_BYTES),
        cost_estimate=BRIEF,
        name="late_down",
    )(bounds, side, adapter_row, pltpu.with_memory_space_constraint(held, pltpu.VMEM), early, *sent)


def up_kernel(owners, rank, adapters, me_ref, side_ref, adapter_ref, up_ref, mine_ref, other_ref, *refs):
    out_refs, held_ref = refs[:-1], refs[-1]
    me, side = me_ref[0], side_ref[0]
    mine, other = mine_ref[...].astype(jnp.float32), other_ref[...].astype(jnp.float32)
    groups = GROUPS // 2
    size = mine.shape[1] // groups
    share = size // owners
    for group in range(GROUPS):
        part, inner = group // groups, group % groups
        span = slice(inner * size, (inner + 1) * size)
        low_rank = jnp.where(side == part, mine[:, span], other[:, span])
        chosen = adapter_ref[0:1, group * size : (group + 1) * size]
        spread = jnp.concatenate(
            [jnp.where(chosen == k, low_rank, 0.0).astype(jnp.bfloat16) for k in range(adapters)],
            axis=0,
        )
        delta = lax.dot_general(up_ref[...], spread, TN, preferred_element_type=jnp.float32)
        delta = delta.astype(jnp.bfloat16)
        for k in range(owners):
            source = (k if part == 0 else lax.rem(me - k + owners, owners)) ^ me
            held_ref[source, :, group * share : (group + 1) * share] = delta[:, k * share : (k + 1) * share]
    for bit, out_ref in enumerate(out_refs):
        out_ref[...] = held_ref[bit]


def up(me, side, adapter_row, up_rows, mine, other, owners):
    rank, wide = mine.shape
    piece = up_rows.shape[1]
    adapters = up_rows.shape[0] // rank
    vmem, smem = pl.BlockSpec(memory_space=pltpu.VMEM), pl.BlockSpec(memory_space=pltpu.SMEM)
    return pl.pallas_call(
        functools.partial(up_kernel, owners, rank, adapters),
        in_specs=[smem, smem, vmem, vmem, vmem, vmem],
        out_shape=[jax.ShapeDtypeStruct((piece, 2 * wide // owners), jnp.bfloat16)] * owners,
        scratch_shapes=[pltpu.VMEM((owners, piece, 2 * wide // owners), jnp.bfloat16)],
        compiler_params=pltpu.CompilerParams(vmem_limit_bytes=VMEM_BYTES),
        cost_estimate=BRIEF,
        name="up",
    )(me, side, adapter_row, up_rows, mine, other)


def tensor_sum(keep, give):
    keep = keep + exchange(give, "tensor", 1)
    keep = keep + exchange(keep, "tensor", 2)
    mine = keep.astype(jnp.bfloat16)
    return mine, exchange(mine, "tensor", 1)


def return_order(owners):
    return [*range(2, owners), 1, 0]


def unpack_kernel(owners, me_ref, place_ref, *refs):
    returned_refs, base_ref, out_ref, held_ref, sem = refs[:owners], *refs[owners:]
    copy = pltpu.make_async_copy(base_ref, held_ref, sem)
    copy.start()
    rows = out_ref.shape[0]
    features, capacity = returned_refs[0].shape
    total = jnp.zeros((features, rows), jnp.float32)
    for k, bit in enumerate(return_order(owners)):
        spot = place_ref[0:1, :] - (me_ref[0] ^ bit) * capacity
        selector = hot(iota((capacity, rows), 0) == spot)
        total += jnp.dot(returned_refs[k][...], selector, preferred_element_type=jnp.float32)
    copy.wait()
    out_ref[...] = (held_ref[...] + ADAPTER_SCALE * total.T).astype(jnp.bfloat16)


def unpack(me, place, returned, base):
    vmem, smem = pl.BlockSpec(memory_space=pltpu.VMEM), pl.BlockSpec(memory_space=pltpu.SMEM)
    return pl.pallas_call(
        functools.partial(unpack_kernel, len(returned)),
        in_specs=[smem, vmem] + [vmem] * len(returned) + [pl.BlockSpec(memory_space=pl.ANY)],
        out_specs=vmem,
        out_shape=pltpu.HBM(base.shape, jnp.bfloat16),
        scratch_shapes=[pltpu.VMEM(base.shape, jnp.float32), pltpu.SemaphoreType.DMA],
        compiler_params=pltpu.CompilerParams(vmem_limit_bytes=VMEM_BYTES),
        cost_estimate=BRIEF,
        name="unpack",
    )(me, place, *returned, base)


def exchange(array, axis, bit):
    size = lax.axis_size(axis)
    return lax.ppermute(array, axis, [(k, k ^ bit) for k in range(size)])


def swap(array):
    return lax.all_to_all(array, "replica", split_axis=0, concat_axis=0, tiled=True)


def body(tokens, value_weight, down_factor, up_factor, request_adapter, adapter_slot_map):
    row_count, quarter = tokens.shape
    owners = lax.axis_size("replica")
    local_adapters, _, rank = down_factor.shape
    half = row_count // owners
    me = lax.axis_index("replica").astype(jnp.int32).reshape(1)
    side = (lax.axis_index("tensor").astype(jnp.int32) % 2).reshape(1)
    requests = request_adapter.reshape(1, -1)
    slot_map = adapter_slot_map.reshape(1, -1)
    down_rows = jnp.swapaxes(down_factor, 1, 2).reshape(local_adapters * rank, quarter)
    up_rows = up_factor.reshape(local_adapters * rank, -1)

    first, over, place, branch = route(me, requests, slot_map, tokens, owners, local_adapters)

    def work(late, place, first, over, tokens, value_weight, down_rows, up_rows, requests, slot_map):
        arrived = swap(first.reshape(owners, half, quarter)).reshape(owners * half, quarter)
        base = base_sum(tokens, value_weight)
        adapter_row, bounds = plan(me, requests, slot_map, owners, local_adapters)
        adapter_row, base = lax.optimization_barrier((adapter_row, base))
        early, held = early_down(bounds, adapter_row, down_rows, arrived, rank, owners)
        keep, give = late_down(bounds, side, adapter_row, held, early, (over, *late), rank, owners)
        mine, other = tensor_sum(keep, give)
        delta = up(me, side, adapter_row, up_rows, mine, other, owners)
        returned = [exchange(delta[bit], "replica", bit) for bit in return_order(owners)[:-1]]
        returned.append(delta[0])
        return unpack(me, place, returned, base)

    def to_one(owner):
        def send(place, first, over, tokens, *rest):
            late = tuple(
                lax.ppermute(over, "replica", [((owner - shift) % owners, owner)])
                for shift in range(1, owners)
            )
            return work(late, place, first, over, tokens, *rest)

        return send

    def to_all(place, first, over, tokens, *rest):
        spot = place[0]
        owner, late = spot // (2 * half), spot % (2 * half) - half
        index = jnp.where(late >= 0, owner * half + late, -1)
        packer = (jnp.arange(owners * half)[:, None] == index[None, :]).astype(jnp.bfloat16)
        outgoing = jnp.dot(packer, tokens, preferred_element_type=jnp.float32)
        outgoing = outgoing.astype(jnp.bfloat16).reshape(owners, half, quarter)
        came = lax.all_to_all(outgoing, "replica", split_axis=0, concat_axis=0, tiled=True)
        here = lax.axis_index("replica")
        late = tuple(
            lax.dynamic_index_in_dim(came, (here - shift) % owners, 0, keepdims=False)
            for shift in range(1, owners)
        )
        return work(late, place, first, over, tokens, *rest)

    return lax.switch(
        branch[0],
        [to_one(owner) for owner in range(owners)] + [to_all],
        place, first, over, tokens, value_weight, down_rows, up_rows, requests, slot_map,
    )


def solution(mesh):
    in_specs = (
        P(("parts", "replica"), "tensor"),
        P("tensor", None),
        P(("parts", "replica"), "tensor", None),
        P(("parts", "replica"), None, "tensor"),
        P("parts"),
        P("parts"),
    )
    out_specs = P(("parts", "replica"), "tensor")
    small = mesh.shape["replica"] in (2, 4, 8) and mesh.shape["tensor"] == 4
    chosen = body if small else plain_body
    return jax.shard_map(chosen, mesh=mesh, in_specs=in_specs, out_specs=out_specs, check_vma=False)
```
